512 devices in a mesh: ctx: 32 (over x, z), ch: 8 (over y), rep: 2 (over core).
Axes of the slice: x: 4, y: 8, z: 8, core: 2. Of those that a mesh axis runs over, the one named last changes fastest.
Arguments:
- projections: bfloat16 [3, 8192, 8192], P(None, 'ctx', ('ch', 'rep')), may hold values from -6 to 6
- short_taps: float32 [3, 3, 8192], P(None, None, ('ch', 'rep')), may hold values from -3 to 3
- skip_gain: float32 [8192], P(('ch', 'rep')), may hold values from 0.5 to 1.5
- long_filter: float32 [8192, 8192], P('ctx', ('ch', 'rep')), may hold values from -3 to 3
- request_ends: int32 [128], replicated, may hold values from 1 to 8191, as said below
- replica_of: int32 [128], replicated, may hold values from 0 to 31, as said below
- slot_index: int32 [128], replicated, may hold values from 0 to 3, as said below
Outputs:
- output: bfloat16 [8192, 8192], P('ctx', ('ch', 'rep'))
- states: bfloat16 [128, 7, 8192], P('ctx')
The draws below stay inside these ranges and needn't reach their ends.
Inputs may be any that keep to these rules, and one draw needn't show every extreme that they name: `request_ends`: every end lies at least one token past the start of its block of 256 tokens; at most 16 ends fall in one such block, and some block holds exactly 16. `replica_of`: each replica receives exactly 4 requests. The pairs (replica_of, slot_index) are all distinct, so every slot is filled once.
All inputs are finite; a program needn't handle non-finite values.
Results may differ from the reference program's by a relative error of at most 0.001.
Values may be sent and summed in bfloat16 or wider, within the bound.
A program may use at most 64 MiB of HBM per device.

```python
import math
import jax
import jax.numpy as jnp
from jax import lax

D = 8192
TOK_DEV = 256
SLOTS = 4
SHORT = 3
SEQ = 8192
N_CTX = 32


def draw_long_filter(key, part):
    key = jax.random.fold_in(key, 11)
    key_rate, key_gain, key_noise = jax.random.split(key, 3)
    log_low = math.log(0.5 / SEQ)
    log_high = math.log(1.0 / 30.0)
    decay_rate = jnp.exp(log_low + (log_high - log_low) * jax.random.uniform(key_rate, (D,), jnp.float32))
    positions = jnp.arange(SEQ, dtype=jnp.float32)[:, None]
    envelope = jnp.exp(-decay_rate[None, :] * positions)
    scale_norm = jnp.sqrt(jnp.expm1(-2.0 * decay_rate) / jnp.expm1(-2.0 * decay_rate * SEQ))
    factor = jnp.exp(jax.random.uniform(key_gain, (D,), jnp.float32, math.log(0.5), math.log(2.0)))
    noise = jnp.clip(jax.random.normal(key_noise, (SEQ, D), jnp.float32), -4.0, 4.0)
    return (noise * envelope * (scale_norm * factor)[None, :]).astype(jnp.float32)


def shared_slots(key):
    return jax.random.permutation(key, N_CTX * SLOTS).astype(jnp.int32)


def draw_replica_of(key, part):
    order = shared_slots(key)
    return (order // SLOTS).astype(jnp.int32)


def draw_slot_index(key, part):
    order = shared_slots(key)
    return (order % SLOTS).astype(jnp.int32)


def draw_request_ends(key, part):
    key = jax.random.fold_in(key, 5)
    key_dev, key_prio, key_mix, key_off = jax.random.split(key, 4)
    most_count = 4 * SLOTS
    dev_pool = jnp.repeat(jnp.arange(N_CTX, dtype=jnp.int32), most_count)
    heavy_dev = jax.random.randint(key_dev, (), 0, N_CTX).astype(jnp.int32)
    priority = jax.random.permutation(key_prio, N_CTX * most_count).astype(jnp.int32)
    priority = jnp.where(dev_pool == heavy_dev, priority - N_CTX * most_count, priority)
    picked = dev_pool[jnp.argsort(priority, stable=True)[:N_CTX * SLOTS]]
    picked = picked[jax.random.permutation(key_mix, N_CTX * SLOTS)]
    offset = jax.random.randint(key_off, (N_CTX * SLOTS,), 1, TOK_DEV).astype(jnp.int32)
    return (picked * TOK_DEV + offset).astype(jnp.int32)


def block_levels(rng, shape, shards, low, top_value):
    def one(dim, blocks):
        heights = jax.random.uniform(jax.random.fold_in(jax.random.fold_in(rng, 6), dim), (blocks,), jnp.float32, low / len(shards), top_value / len(shards))
        return jnp.repeat(jnp.exp(heights), shape[dim] // blocks).reshape((-1,) + (1,) * (len(shape) - dim - 1))

    factor_of = one(*shards[0])
    for cut in shards[1:]:
        factor_of = factor_of * one(*cut)
    return factor_of


def gaussian(stream_key, shape, scale, limit, cuts=(), kind=jnp.bfloat16):
    gain = block_levels(stream_key, shape, cuts, -0.22, 0.18) if cuts else 1.0
    entries = jax.random.normal(stream_key, shape, jnp.float32) * scale * gain
    return jnp.minimum(jnp.maximum(entries, -limit), limit).astype(kind)


def setup_inputs(seed: int = 0) -> dict:
    key_of = jax.random.split(jax.random.key(seed), 8)
    return {
        "projections": gaussian(key_of[0], (3, SEQ, D), 1.0, 6.0, ((1, 32), (2, 16))),
        "short_taps": gaussian(key_of[1], (3, SHORT, D), 0.6, 3.0, ((2, 16),), jnp.float32),
        "skip_gain": jnp.clip(0.5 + 1.0 * jax.random.uniform(key_of[2], (D,), jnp.float32) ** block_levels(key_of[2], (D,), ((0, 16),), -0.2, 0.2), 0.5, 1.5),
        "long_filter": draw_long_filter(jax.random.fold_in(key_of[7], 71), 0),
        "request_ends": draw_request_ends(jax.random.fold_in(key_of[7], 71), 0),
        "replica_of": draw_replica_of(jax.random.fold_in(key_of[7], 71), 0),
        "slot_index": draw_slot_index(jax.random.fold_in(key_of[7], 71), 0),
    }


def short_conv(projections, short_taps):
    values = projections.astype(jnp.float32)
    count = values.shape[1]
    padded = jnp.pad(values, ((0, 0), (2, 0), (0, 0)))
    return (short_taps[:, 0, None, :] * padded[:, 2:]
            + short_taps[:, 1, None, :] * padded[:, 1:count + 1]
            + short_taps[:, 2, None, :] * padded[:, :count])


def long_conv(signal, long_filter):
    width = min(D, 512)
    groups = D // width
    sig_blocks = signal.reshape(SEQ, groups, width).transpose(1, 0, 2)
    filt_blocks = long_filter.reshape(SEQ, groups, width).transpose(1, 0, 2)

    def one_block(pair):
        sig_part, filt_part = pair
        spectrum = jnp.fft.rfft(sig_part, n=2 * SEQ, axis=0) * jnp.fft.rfft(filt_part, n=2 * SEQ, axis=0)
        return jnp.fft.irfft(spectrum, n=2 * SEQ, axis=0)[:SEQ].astype(sig_part.dtype)

    mixed = lax.map(one_block, (sig_blocks, filt_blocks))
    return mixed.transpose(1, 0, 2).reshape(SEQ, D)


def reference(projections, short_taps, skip_gain, long_filter, request_ends, replica_of, slot_index):
    conv = short_conv(projections, short_taps)
    signal = conv[1] * conv[2]
    mixed = long_conv(signal, long_filter)
    output = (conv[0] * (mixed + skip_gain[None, :] * signal)).astype(jnp.bfloat16)
    prev_rows = projections[:, request_ends - 1]
    cur_rows = projections[:, request_ends]
    request_state = jnp.stack([prev_rows[0], cur_rows[0], prev_rows[1], cur_rows[1],
                               prev_rows[2], cur_rows[2], output[request_ends]], axis=1)
    target = replica_of * SLOTS + slot_index
    states = jnp.zeros((N_CTX * SLOTS, 7, D), jnp.bfloat16).at[target].set(request_state)
    return output, states
```

```python
import math

import jax
import jax.numpy as jnp
import ml_dtypes
import numpy as np
from jax import lax
from jax.experimental import pallas as pl
from jax.experimental.pallas import tpu as pltpu
from jax.sharding import PartitionSpec as P

MESH = pl.DeviceIdType.MESH
F32 = jnp.float32
BF16 = jnp.bfloat16

N_CTX = 32
CH = 16
TOK = 256
SEQ = 8192
LEN_A = 64
LEN_B = 128
SLOTS = 4


def split_np(table):
    high = table.astype(ml_dtypes.bfloat16)
    low = (table - high.astype(np.float64)).astype(ml_dtypes.bfloat16)
    return high, low


def tables():
    k = np.arange(LEN_A) + 0.25
    theta = 2.0 * np.pi * np.outer(k, np.arange(LEN_A)) / LEN_A
    outer = np.concatenate([np.cos(theta), -np.sin(theta)], axis=0)
    o_high, o_low = split_np(outer)
    first = np.concatenate([o_high, o_high, o_low], axis=1)
    e_high, e_low = split_np(outer.T / SEQ)
    last = np.concatenate([e_high, e_low], axis=1)
    phi = 2.0 * np.pi * np.outer(np.arange(LEN_B), np.arange(LEN_B)) / LEN_B
    c, s = np.cos(phi), np.sin(phi)
    inner = np.block([[c, -s], [s, c]])
    i_high, i_low = split_np(inner)
    v_high, v_low = split_np(inner.T)
    inner_all = np.stack([i_high, i_low, v_high, v_low])
    turn = 2.0 * np.pi * np.outer(k, np.arange(LEN_B)) / SEQ
    turns = np.stack([np.tile(np.cos(turn), (1, 2)), np.tile(np.sin(turn), (1, 2))]).astype(np.float32)
    row, col = np.arange(256)[:, None], np.arange(512)[None, :]
    place = np.stack(
        [(row % 128 == col // 4) & (row // 128 + 2 * p == col % 4) for p in (0, 1)]
    ).astype(ml_dtypes.bfloat16)
    return first, last, inner_all, turns, place


def split(value):
    high = value.astype(BF16)
    return high, (value - high.astype(F32)).astype(BF16)


def dot(a, b):
    return jnp.dot(a, b, preferred_element_type=F32)


def kernel(
    proj_hbm, filt_hbm, taps_ref, gain_ref, ends_ref, repl_ref, slot_ref,
    first_ref, last_ref, inner_ref, turns_ref, place_ref,
    out_ref, states_ref,
    proj, filt, f_send, kv_send, q_send, o_send, e_send, l_send,
    f_recv, kv_recv, q_recv, o_recv, e_recv, l_recv, ge_recv, gl_recv,
    spec, sig, mixed, onehot, taps_t, tmp,
    local_sem, send_sem, recv_sem,
):
    me = lax.axis_index("ctx")
    ch, rep = lax.axis_index("ch"), lax.axis_index("rep")
    mine = ch * 2 + rep

    load_f = pltpu.make_async_copy(filt_hbm, filt, local_sem.at[0])
    load_p = pltpu.make_async_copy(proj_hbm, proj, local_sem.at[1])
    load_f.start()
    load_p.start()

    barrier = pltpu.get_barrier_semaphore()

    def greet_ctx(t, carry):
        pl.semaphore_signal(
            barrier, inc=1, device_id={"ctx": lax.rem(me + t, N_CTX)}, device_id_type=MESH
        )
        return carry

    def near(t):
        other = lax.rem(mine + t, 16)
        return {"ch": other // 2, "rep": lax.rem(other, 2)}

    def greet_near(t, carry):
        pl.semaphore_signal(barrier, inc=1, device_id=near(t), device_id_type=MESH)
        return carry

    lax.fori_loop(1, N_CTX, greet_ctx, 0)
    lax.fori_loop(1, 16, greet_near, 0)

    def send_ctx(n, source, target):
        def one(t, carry):
            peer = lax.rem(me + t, N_CTX)
            pltpu.make_async_remote_copy(
                src_ref=source(peer), dst_ref=target.at[me],
                send_sem=send_sem.at[n], recv_sem=recv_sem.at[n],
                device_id={"ctx": peer}, device_id_type=MESH,
            ).start()
            return carry

        lax.fori_loop(1, N_CTX, one, 0)

    def send_near(n, buffer):
        def one(t, carry):
            pltpu.make_async_remote_copy(
                src_ref=buffer.at[mine], dst_ref=buffer.at[mine],
                send_sem=send_sem.at[n], recv_sem=recv_sem.at[n],
                device_id=near(t), device_id_type=MESH,
            ).start()
            return carry

        lax.fori_loop(1, 16, one, 0)

    def await_bytes(buffer, count, sem):
        part = buffer.at[pl.ds(0, count)]
        pltpu.make_async_copy(part, part, sem).wait()

    load_f.wait()
    for g in range(4):
        block = filt[:, 128 * g : 128 * g + 128].T
        for h in range(2):
            f_send[8 * g : 8 * g + 8, CH * h : CH * h + CH] = (
                block[:, 128 * h : 128 * h + 128].reshape(8, CH, 128)
            )
    pl.semaphore_wait(barrier, N_CTX - 1 + 15)
    send_ctx(0, lambda peer: f_send.at[peer], f_recv)
    f_recv[me] = f_send[me]

    load_p.wait()
    for p in (1, 2):
        for g in range(4):
            kv_send[8 * g : 8 * g + 8, 16 * (p - 1) : 16 * p] = (
                proj[p, :, 128 * g : 128 * g + 128].T.reshape(8, CH, TOK)
            )
    send_ctx(1, lambda peer: kv_send.at[peer], kv_recv)
    kv_recv[me] = kv_send[me]
    for g in range(4):
        q_send[8 * g : 8 * g + 8] = proj[0, :, 128 * g : 128 * g + 128].T.reshape(8, CH, TOK)
    send_ctx(2, lambda peer: q_send.at[peer], q_recv)
    q_recv[me] = q_send[me]

    rows = [taps_ref[p] for p in range(3)] + [gain_ref[...], jnp.zeros((6, 512), F32)]
    taps_t[...] = jnp.concatenate(rows, axis=0).T
    my_taps = taps_t[pl.ds(pl.multiple_of(me * CH, CH), CH), :]

    def column(n):
        return jnp.broadcast_to(my_taps[:, n : n + 1], (CH, TOK))

    target = repl_ref[...] * SLOTS + slot_ref[...]
    target_rows = jnp.broadcast_to(target, (128, 128)).T
    ends_rows = jnp.broadcast_to(ends_ref[...], (128, 128)).T
    slots_here = lax.broadcasted_iota(jnp.int32, (128, 128), 1)
    by_slot = jnp.sum(jnp.where(target_rows == slots_here, ends_rows, 0), axis=0, keepdims=True)
    wanted = jnp.concatenate([by_slot - 1, by_slot], axis=1)
    token = lax.broadcasted_iota(jnp.int32, (TOK, 256), 0)

    def pick(i, carry):
        onehot[i] = jnp.where(token + i * TOK == wanted, 1.0, 0.0).astype(BF16)
        return carry

    lax.fori_loop(0, N_CTX, pick, 0)

    cos_t, sin_t = turns_ref[0], turns_ref[1]

    def forward(ref, c):
        x = jnp.concatenate(
            [ref[pl.ds(c + n, LEN_A, stride=CH), :] for n in range(2)], axis=1
        )
        high, low = split(x)
        z = dot(first_ref[...], jnp.concatenate([high, low, high], axis=0))
        re, im = z[:64], z[64:]
        zr = re * cos_t + im * sin_t
        zi = im * cos_t - re * sin_t
        z = jnp.concatenate(
            [
                jnp.concatenate([zr[:, :128], zi[:, :128]], axis=1),
                jnp.concatenate([zr[:, 128:], zi[:, 128:]], axis=1),
            ],
            axis=0,
        )
        high, low = split(z)
        return dot(high, inner_ref[0]) + (dot(low, inner_ref[0]) + dot(high, inner_ref[1]))

    await_bytes(f_recv, N_CTX - 1, recv_sem.at[0])
    flat_f = f_recv.reshape(LEN_A * CH, 128)

    def filter_pair(m, carry):
        spec[pl.ds(pl.multiple_of(128 * m, 128), 128), :] = forward(flat_f, 2 * m)
        return carry

    lax.fori_loop(0, CH // 2, filter_pair, 0)

    lane = lax.broadcasted_iota(jnp.int32, (2 * CH, TOK), 1)
    kv_taps = [jnp.concatenate([column(3 + j), column(6 + j)], axis=0) for j in range(3)]
    await_bytes(kv_recv, N_CTX - 1, recv_sem.at[1])

    def signal_block(i, carry):
        before1, before2 = carry
        x = kv_recv[i].astype(F32)
        roll1, roll2 = pltpu.roll(x, 1, 1), pltpu.roll(x, 2, 1)
        conv = (
            kv_taps[0] * x
            + kv_taps[1] * jnp.where(lane < 1, before1, roll1)
            + kv_taps[2] * jnp.where(lane < 2, before2, roll2)
        )
        signal = conv[:CH] * conv[CH:]
        sig[pl.ds(pl.multiple_of(i * 2 * CH, 2 * CH), 2 * CH), :] = jnp.concatenate(
            [signal[:, :128], signal[:, 128:]], axis=0
        )
        return roll1, roll2

    zero = jnp.zeros((2 * CH, TOK), F32)
    lax.fori_loop(0, N_CTX, signal_block, (zero, zero))

    def gather_kv(i, total):
        return total + dot(kv_recv[i], onehot[i])

    rows_kv = lax.fori_loop(0, N_CTX, gather_kv, jnp.zeros((2 * CH, 256), F32)).astype(BF16)
    early = dot(rows_kv[:CH], place_ref[0]) + dot(rows_kv[CH:], place_ref[1])
    for g in range(4):
        e_send[g] = early[:, 128 * g : 128 * g + 128].astype(BF16)
    send_ctx(3, lambda peer: e_send.at[peer // 8], e_recv)
    e_recv[me] = e_send[me // 8]

    def convolve_pair(m, carry):
        x = forward(sig, 2 * m)
        f = spec[pl.ds(pl.multiple_of(128 * m, 128), 128), :]
        xr, xi, fr, fi = x[:, :128], x[:, 128:], f[:, :128], f[:, 128:]
        y = jnp.concatenate([xr * fr - xi * fi, xr * fi + xi * fr], axis=1)
        high, low = split(y)
        u = dot(high, inner_ref[2]) + (dot(low, inner_ref[2]) + dot(high, inner_ref[3]))
        ur = jnp.concatenate([u[:64, :128], u[64:, :128]], axis=1)
        ui = jnp.concatenate([u[:64, 128:], u[64:, 128:]], axis=1)
        w = jnp.concatenate([ur * cos_t - ui * sin_t, ui * cos_t + ur * sin_t], axis=0)
        high, low = split(w)
        y = dot(last_ref[...], jnp.concatenate([high, high], axis=0)) + dot(last_ref[:, :128], low)
        mixed[pl.ds(2 * m, LEN_A, stride=CH), :] = y[:, :128]
        mixed[pl.ds(2 * m + 1, LEN_A, stride=CH), :] = y[:, 128:]
        return carry

    lax.fori_loop(0, CH // 2, convolve_pair, 0)

    q_taps = [column(j) for j in range(3)]
    gain = column(9)
    lane_q = lax.broadcasted_iota(jnp.int32, (CH, TOK), 1)
    await_bytes(q_recv, N_CTX - 1, recv_sem.at[2])

    def gate_block(i, carry):
        before1, before2 = carry
        x = q_recv[i].astype(F32)
        roll1, roll2 = pltpu.roll(x, 1, 1), pltpu.roll(x, 2, 1)
        conv = (
            q_taps[0] * x
            + q_taps[1] * jnp.where(lane_q < 1, before1, roll1)
            + q_taps[2] * jnp.where(lane_q < 2, before2, roll2)
        )
        for h in range(2):
            here = pl.ds(pl.multiple_of((2 * i + h) * CH, CH), CH)
            half = slice(128 * h, 128 * h + 128)
            o_send[i, :, half] = (
                conv[:, half] * (mixed[here, :] + gain[:, half] * sig[here, :])
            ).astype(BF16)
        return roll1, roll2

    zero_q = jnp.zeros((CH, TOK), F32)
    lax.fori_loop(0, N_CTX, gate_block, (zero_q, zero_q))

    def gather_q(i, total):
        both = jnp.concatenate([q_recv[i], o_send[i]], axis=0)
        return total + dot(both, onehot[i])

    rows_q = lax.fori_loop(0, N_CTX, gather_q, jnp.zeros((2 * CH, 256), F32)).astype(BF16)
    late = dot(rows_q[:CH], place_ref[0]) + dot(rows_q[CH:, 128:], place_ref[1, :128])
    for g in range(4):
        l_send[g] = late[:, 128 * g : 128 * g + 128].astype(BF16)
    send_ctx(4, lambda peer: l_send.at[peer // 8], l_recv)
    send_ctx(5, lambda peer: o_send.at[peer], o_recv)
    l_recv[me] = l_send[me // 8]
    o_recv[me] = o_send[me]

    mine_rows = pl.ds(pl.multiple_of(lax.rem(me, 8) * 16, 16), 16)

    def own_rows(received):
        tmp[...] = received[...].reshape(N_CTX * CH, 128).astype(F32).T
        return tmp[mine_rows, :].astype(BF16)

    await_bytes(e_recv, N_CTX - 1, recv_sem.at[3])
    ge_recv[mine] = own_rows(e_recv)
    send_near(6, ge_recv)
    await_bytes(l_recv, N_CTX - 1, recv_sem.at[4])
    gl_recv[mine] = own_rows(l_recv)
    send_near(7, gl_recv)

    await_bytes(o_recv, N_CTX - 1, recv_sem.at[5])
    for g in range(4):
        out_ref[:, 128 * g : 128 * g + 128] = o_recv[8 * g : 8 * g + 8].reshape(128, TOK).T

    await_bytes(ge_recv, 15, recv_sem.at[6])
    await_bytes(gl_recv, 15, recv_sem.at[7])
    for j in range(16):
        kv, qo = ge_recv[j].astype(F32), gl_recv[j].astype(F32)
        for s in range(SLOTS):
            r = 4 * s
            block = jnp.concatenate([qo[r : r + 2], kv[r : r + 4], qo[r + 2 : r + 3]], axis=0)
            states_ref[s, :, 512 * j : 512 * j + 512] = block.astype(BF16)

    await_bytes(f_send, N_CTX - 1, send_sem.at[0])
    await_bytes(kv_send, N_CTX - 1, send_sem.at[1])
    await_bytes(q_send, N_CTX - 1, send_sem.at[2])
    await_bytes(e_recv, N_CTX - 1, send_sem.at[3])
    await_bytes(l_recv, N_CTX - 1, send_sem.at[4])
    await_bytes(o_send, N_CTX - 1, send_sem.at[5])
    await_bytes(ge_recv, 15, send_sem.at[6])
    await_bytes(gl_recv, 15, send_sem.at[7])


def body(projections, short_taps, skip_gain, long_filter, request_ends, replica_of, slot_index):
    first, last, inner, turns, place = tables()
    whole = pl.BlockSpec(memory_space=pltpu.VMEM)
    hbm = pl.BlockSpec(memory_space=pl.ANY)

    def blocks(rows, lanes, dtype, count=N_CTX):
        return pltpu.VMEM((count, rows, lanes), dtype)

    return pl.pallas_call(
        kernel,
        out_shape=(
            jax.ShapeDtypeStruct((TOK, 512), BF16),
            jax.ShapeDtypeStruct((SLOTS, 7, 8192), BF16),
        ),
        in_specs=[hbm, hbm] + [whole] * 10,
        out_specs=(whole, whole),
        scratch_shapes=[
            pltpu.VMEM((3, TOK, 512), BF16),
            pltpu.VMEM((TOK, 512), F32),
            blocks(2 * CH, 128, F32), blocks(2 * CH, TOK, BF16), blocks(CH, TOK, BF16), blocks(CH, TOK, BF16),
            blocks(CH, 128, BF16, 4), blocks(CH, 128, BF16, 4),
            blocks(2 * CH, 128, F32), blocks(2 * CH, TOK, BF16), blocks(CH, TOK, BF16), blocks(CH, TOK, BF16),
            blocks(CH, 128, BF16), blocks(CH, 128, BF16),
            blocks(16, 512, BF16, 16), blocks(16, 512, BF16, 16),
            pltpu.VMEM((64 * CH, 256), F32),
            pltpu.VMEM((LEN_A * CH, 128), F32),
            pltpu.VMEM((LEN_A * CH, 128), F32),
            blocks(TOK, 256, BF16),
            pltpu.VMEM((512, 16), F32),
            pltpu.VMEM((128, 512), F32),
            pltpu.SemaphoreType.DMA((2,)),
            pltpu.SemaphoreType.DMA((8,)),
            pltpu.SemaphoreType.DMA((8,)),
        ],
        compiler_params=pltpu.CompilerParams(
            collective_id=0, has_side_effects=True, vmem_limit_bytes=48 * 2**20
        ),
        cost_estimate=pl.CostEstimate(flops=2 * 10**9, bytes_accessed=4 * 10**6, transcendentals=0),
    )(
        projections, long_filter, short_taps, skip_gain.reshape(1, 512),
        request_ends.reshape(1, 128), replica_of.reshape(1, 128), slot_index.reshape(1, 128),
        jnp.asarray(first), jnp.asarray(last), jnp.asarray(inner), jnp.asarray(turns), jnp.asarray(place),
    )


def solution(mesh):
    return jax.shard_map(
        body,
        mesh=mesh,
        in_specs=(
            P(None, "ctx", ("ch", "rep")),
            P(None, None, ("ch", "rep")),
            P(("ch", "rep")),
            P("ctx", ("ch", "rep")),
            P(),
            P(),
            P(),
        ),
        out_specs=(P("ctx", ("ch", "rep")), P("ctx", None, None)),
        check_vma=False,
    )
```

```python
import math

import jax
import jax.numpy as jnp
import ml_dtypes
import numpy as np
from jax import lax
from jax.experimental import pallas as pl
from jax.experimental.pallas import tpu as pltpu
from jax.sharding import PartitionSpec as P

MESH = pl.DeviceIdType.MESH
F32 = jnp.float32
BF16 = jnp.bfloat16

N_CTX = 32
CH = 16
TOK = 256
SEQ = 8192
LEN_A = 64
LEN_B = 128
SLOTS = 4
TOP = 32767.0


def split_np(table):
    high = table.astype(ml_dtypes.bfloat16)
    low = (table - high.astype(np.float64)).astype(ml_dtypes.bfloat16)
    return high, low


def tables():
    k = np.arange(LEN_A) + 0.25
    theta = 2.0 * np.pi * np.outer(k, np.arange(LEN_A)) / LEN_A
    outer = np.concatenate([np.cos(theta), -np.sin(theta)], axis=0)
    o_high, o_low = split_np(outer)
    first = np.concatenate([o_high, o_high, o_low], axis=1)
    e_high, e_low = split_np(outer.T / SEQ)
    last = np.concatenate([e_high, e_low], axis=1)
    phi = 2.0 * np.pi * np.outer(np.arange(LEN_B), np.arange(LEN_B)) / LEN_B
    c, s = np.cos(phi), np.sin(phi)
    inner = np.block([[c, -s], [s, c]])
    i_high, i_low = split_np(inner)
    v_high, v_low = split_np(inner.T)
    inner_all = np.stack([i_high, i_low, v_high, v_low])
    turn = 2.0 * np.pi * np.outer(k, np.arange(LEN_B)) / SEQ
    turns = np.stack([np.tile(np.cos(turn), (1, 2)), np.tile(np.sin(turn), (1, 2))]).astype(np.float32)
    return first, last, inner_all, turns


def row_scale(block, axis):
    largest = jnp.max(jnp.abs(block), axis=axis, keepdims=True)
    step = jnp.maximum(largest, 2.0**-100) * (1.0078125 / TOP)
    return step.astype(BF16).astype(F32)


def code(scaled):
    return jnp.floor(scaled + 0.5).astype(jnp.int32).astype(jnp.int16)


def decode(codes):
    return codes.astype(jnp.int32).astype(F32)


def iota(shape, axis):
    return lax.broadcasted_iota(jnp.int32, shape, axis)


def split(value):
    high = value.astype(BF16)
    return high, (value - high.astype(F32)).astype(BF16)


def dot(a, b):
    return jnp.dot(a, b, preferred_element_type=F32)


def kernel(*refs):
    hbm_refs, (out_ref, states_ref), vmem_refs = refs[:11], refs[11:13], refs[13:24]
    (
        proj, filt, taps_ref, gain_ref, ends_ref, repl_ref, slot_ref,
        first_ref, last_ref, inner_ref, turns_ref,
    ) = vmem_refs
    (
        halo_send, halo_recv, f_send, s_send, m_send, r_send, e_send, l_send,
        f_recv, s_recv, m_recv, r_recv, e_recv, l_recv, ge_recv, gl_recv,
        spec, filter_t, sig_t, mixed, query, signal, steps, onehot, taps_t, tmp,
        local_sem, send_sem, recv_sem,
    ) = refs[24:]
    me = lax.axis_index("ctx")
    ch, rep = lax.axis_index("ch"), lax.axis_index("rep")
    my_x, my_z = me // 8, lax.rem(me, 8)
    after = {"ctx": lax.rem(me + 1, N_CTX)}
    sibling = {"rep": 1 - rep}

    loads = [
        pltpu.make_async_copy(source, target, local_sem.at[n])
        for n, (source, target) in enumerate(zip(hbm_refs, vmem_refs))
    ]
    for load in loads:
        load.start()

    barrier = pltpu.get_barrier_semaphore()

    def greet(device):
        pl.semaphore_signal(barrier, inc=1, device_id=device, device_id_type=MESH)

    def greet_ctx(t, carry):
        greet({"ctx": lax.rem(me + t, N_CTX)})
        return carry

    def greet_ch(t, carry):
        greet({"ch": lax.rem(ch + t, 8)})
        return carry

    lax.fori_loop(1, N_CTX, greet_ctx, 0)
    lax.fori_loop(1, 8, greet_ch, 0)
    greet(sibling)

    def remote(n, source, target, device):
        return pltpu.make_async_remote_copy(
            src_ref=source, dst_ref=target,
            send_sem=send_sem.at[n], recv_sem=recv_sem.at[n],
            device_id=device, device_id_type=MESH,
        )

    def send_line(n, source, target, dx):
        x = lax.rem(my_x + dx, 4)

        def one(t, carry):
            peer = 8 * x + lax.rem(my_z + t, 8)
            remote(n, source(peer), target.at[me], {"ctx": peer}).start()
            return carry

        lax.fori_loop(1 if dx == 0 else 0, 8, one, 0)

    def send_ctx(n, source, target):
        for dx in range(4):
            send_line(n, source, target, dx)

    def send_ch(n, buffer):
        def one(t, carry):
            remote(n, buffer.at[rep, ch], buffer.at[rep, ch], {"ch": lax.rem(ch + t, 8)}).start()
            return carry

        lax.fori_loop(1, 8, one, 0)

    def await_bytes(part, sem):
        pltpu.make_async_copy(part, part, sem).wait()

    def others(buffer):
        return buffer.at[pl.ds(0, N_CTX - 1)]

    def seven(buffer):
        return buffer.at[0, pl.ds(0, 7)]

    def column_block(dx):
        g = lax.rem(my_x + dx, 4)
        return pl.ds(pl.multiple_of(8 * g, 8), 8), pl.ds(pl.multiple_of(128 * g, 128), 128)

    def put_codes(block, kind, dx, target):
        devices, lanes = column_block(dx)
        step = row_scale(block, 0)
        steps[kind : kind + 1, lanes] = step
        turned = (block * (1.0 / step)).T
        for h in range(2):
            target[devices, CH * h : CH * h + CH] = code(
                turned[:, 128 * h : 128 * h + 128]
            ).reshape(8, CH, 128)

    def put_filter(dx):
        put_codes(filt[:, column_block(dx)[1]], 0, dx, f_send)

    loads[0].wait()
    halo_send[...] = jnp.concatenate(
        [proj[p, TOK - 16 :, :].astype(F32)[14:] for p in range(3)] + [jnp.zeros((2, 512), F32)], axis=0
    )
    steps[...] = jnp.zeros((8, 512), F32)
    loads[1].wait()
    put_filter(0)
    pl.semaphore_wait(barrier, N_CTX - 1 + 7 + 1)
    halo_copy = remote(0, halo_send, halo_recv, after)
    halo_copy.start()
    for dx in range(4):
        if dx > 0:
            put_filter(dx)
        send_line(1, lambda peer: f_send.at[peer], f_recv, dx)
    f_recv[me] = f_send[me]
    for load in loads[2:]:
        load.wait()

    ends = ends_ref[...]
    end_block = ends // TOK
    end_lane = ends - end_block * TOK

    def down(row):
        return jnp.broadcast_to(row, (128, 128)).T

    earlier = iota((128, 128), 0) < iota((128, 128), 1)
    same = down(end_block) == end_block
    rank = jnp.sum(jnp.where(earlier, jnp.where(same, 1, 0), 0), axis=0, keepdims=True)
    slot_of = down(repl_ref[...] * SLOTS + slot_ref[...])

    def at_slot(row, slots):
        values = down(row)[:, :1]
        hit = slot_of[:, :1] == slots
        return jnp.sum(jnp.where(hit, values, 0), axis=0, keepdims=True)

    where_code = end_block * 16 + rank
    column = iota((128, 1024), 1)
    e_code = at_slot(where_code, column // 32 * 4 + column % 4)
    slots_row = iota((128, 128), 1)
    t_code = at_slot(where_code, slots_row)
    t_end = at_slot(ends, slots_row)
    row_kind = iota((1, 1024), 1) % 32 // 4
    code_all = jnp.concatenate([e_code, t_code, t_code, t_code], axis=1)
    kind_all = jnp.concatenate(
        [jnp.where(row_kind < 6, row_kind + 1, -10)] + [jnp.full((1, 128), k, jnp.int32) for k in range(3)],
        axis=1,
    )
    block_all = code_all // 16
    lane_all = kind_all * 16 + (code_all - block_all * 16)
    onehot[...] = jnp.where(iota((128, 1408), 0) == lane_all, 1.0, 0.0).astype(BF16)

    mine = jnp.where(end_block == me, jnp.where(rank == iota((16, 128), 0), end_lane + 100, 0), 0)
    place = jnp.sum(mine, axis=1, keepdims=True) - 100
    token = iota((16, TOK), 1)

    def rows_at(back):
        return jnp.where(token == place - back, 1.0, 0.0).astype(BF16)

    two_rows = jnp.concatenate([rows_at(1), rows_at(0)], axis=0)
    three_rows = jnp.concatenate([rows_at(2), two_rows], axis=0)

    halo_copy.wait_recv()
    token_row = iota((TOK, 128), 0)
    for dx in range(4):
        devices, lanes = column_block(dx)
        conv = []
        halo_here = jnp.where(me > 0, halo_recv[:, lanes], 0.0)
        for p in range(3):
            x = proj[p, :, lanes].astype(F32)
            tail2, tail1 = halo_here[2 * p : 2 * p + 1], halo_here[2 * p + 1 : 2 * p + 2]
            back1 = jnp.where(token_row < 1, tail1, pltpu.roll(x, 1, 0))
            back2 = jnp.where(
                token_row < 1, tail2, jnp.where(token_row < 2, tail1, pltpu.roll(x, 2, 0))
            )
            taps = taps_ref[p, :, lanes]
            conv.append(taps[0:1] * x + taps[1:2] * back1 + taps[2:3] * back2)
        query[:, lanes] = conv[0]
        product = conv[1] * conv[2]
        signal[:, lanes] = product
        put_codes(product, 1, dx, s_send)
        q_rows = dot(three_rows, proj[0, :, lanes])
        first_rows = q_rows[:16] + jnp.where(place == 1, halo_here[1:2], 0.0)
        rows = jnp.concatenate(
            [
                first_rows, q_rows[16:], dot(two_rows, proj[1, :, lanes]), dot(two_rows, proj[2, :, lanes]),
                steps[:, lanes], jnp.zeros((8, 128), F32),
            ],
            axis=0,
        )
        r_send[devices] = rows.T.astype(BF16).reshape(8, CH, 128)
        send_line(2, lambda peer: r_send.at[peer], r_recv, dx)
    r_recv[me] = r_send[me]
    send_ctx(3, lambda peer: s_send.at[peer], s_recv)
    s_recv[me] = s_send[me]

    rows = [taps_ref[p] for p in range(3)] + [gain_ref[...], jnp.zeros((6, 512), F32)]
    taps_t[...] = jnp.concatenate(rows, axis=0).T
    my_taps = taps_t[pl.ds(pl.multiple_of(me * CH, CH), CH), :]

    cos_t, sin_t = turns_ref[0], turns_ref[1]

    def read_codes(received, target, lane):
        def one(i, carry):
            step = r_recv[i].astype(F32)[:, lane : lane + 1]
            step = jnp.concatenate([step, step], axis=0)
            target[pl.ds(pl.multiple_of(i * 32, 32), 32), :] = decode(received[i]) * step
            return carry

        lax.fori_loop(0, N_CTX, one, 0, unroll=4)

    def forward(ref, c):
        x = jnp.concatenate(
            [ref[pl.ds(c + n, LEN_A, stride=CH), :] for n in range(2)], axis=1
        )
        high, low = split(x)
        z = dot(first_ref[...], jnp.concatenate([high, low, high], axis=0))
        re, im = z[:64], z[64:]
        zr = re * cos_t + im * sin_t
        zi = im * cos_t - re * sin_t
        z = jnp.concatenate(
            [
                jnp.concatenate([zr[:, :128], zi[:, :128]], axis=1),
                jnp.concatenate([zr[:, 128:], zi[:, 128:]], axis=1),
            ],
            axis=0,
        )
        high, low = split(z)
        return dot(high, inner_ref[0]) + (dot(low, inner_ref[0]) + dot(high, inner_ref[1]))

    await_bytes(others(f_recv), recv_sem.at[1])
    await_bytes(others(r_recv), recv_sem.at[2])
    read_codes(f_recv, filter_t, 112)

    def filter_pair(m, carry):
        spec[pl.ds(pl.multiple_of(128 * m, 128), 128), :] = forward(filter_t, 2 * m)
        return carry

    lax.fori_loop(0, CH // 2, filter_pair, 0, unroll=2)

    def gather_four(i, total):
        blocks = r_recv[pl.ds(pl.multiple_of(4 * i, 4), 4)].reshape(4 * CH, 128)
        found = dot(blocks, onehot[...])
        for u in range(4):
            total = total + jnp.where(block_all == 4 * i + u, found[CH * u : CH * u + CH], 0.0)
        return total

    wanted = lax.fori_loop(0, N_CTX // 4, gather_four, jnp.zeros((CH, 1408), F32))
    for g in range(8):
        e_send[g] = wanted[:, 128 * g : 128 * g + 128].astype(BF16)
    send_ctx(4, lambda peer: e_send.at[peer // 4], e_recv)
    e_recv[me] = e_send[me // 4]
    q_end = (
        my_taps[:, 2:3] * wanted[:, 1024:1152]
        + my_taps[:, 1:2] * wanted[:, 1152:1280]
        + my_taps[:, 0:1] * wanted[:, 1280:1408]
    )

    await_bytes(others(s_recv), recv_sem.at[3])
    read_codes(s_recv, sig_t, 113)

    def convolve_pair(m, carry):
        x = forward(sig_t, 2 * m)
        f = spec[pl.ds(pl.multiple_of(128 * m, 128), 128), :]
        xr, xi, fr, fi = x[:, :128], x[:, 128:], f[:, :128], f[:, 128:]
        y = jnp.concatenate([xr * fr - xi * fi, xr * fi + xi * fr], axis=1)
        high, low = split(y)
        u = dot(high, inner_ref[2]) + (dot(low, inner_ref[2]) + dot(high, inner_ref[3]))
        ur = jnp.concatenate([u[:64, :128], u[64:, :128]], axis=1)
        ui = jnp.concatenate([u[:64, 128:], u[64:, 128:]], axis=1)
        w = jnp.concatenate([ur * cos_t - ui * sin_t, ui * cos_t + ur * sin_t], axis=0)
        high, low = split(w)
        y = dot(last_ref[...], jnp.concatenate([high, high], axis=0)) + dot(last_ref[:, :128], low)
        mixed[pl.ds(2 * m, LEN_A, stride=CH), :] = y[:, :128]
        mixed[pl.ds(2 * m + 1, LEN_A, stride=CH), :] = y[:, 128:]
        return carry

    lax.fori_loop(0, CH // 2, convolve_pair, 0, unroll=4)

    lane = iota((CH, 128), 1)
    end_half = t_end // 128
    end_spot = t_end - end_half * 128
    spot = jnp.where(iota((128, 128), 0) == end_spot, 1.0, 0.0).astype(BF16)
    spots = jnp.concatenate([spot, spot], axis=0)
    gain_col = my_taps[:, 9:10]
    gain_col = jnp.concatenate([gain_col, gain_col], axis=0)

    def finish_block(i, carry):
        ended, tiles = carry
        here = pl.ds(pl.multiple_of(i * 32, 32), 32)
        y = mixed[here, :]
        high, low = split(y + gain_col * sig_t[here, :])
        found = dot(jnp.concatenate([high, low], axis=1), spots)
        ended = ended + jnp.where(end_half == 2 * i, found[:CH], 0.0)
        ended = ended + jnp.where(end_half == 2 * i + 1, found[CH:], 0.0)
        step = row_scale(jnp.maximum(jnp.abs(y[:CH]), jnp.abs(y[CH:])), 1)
        both = jnp.concatenate([step, step], axis=0)
        m_send[i] = code(y * (1.0 / both))
        tiles = jnp.where(lane == 32 + i, step, tiles)
        return ended, tiles

    empty = jnp.zeros((CH, 128), F32)
    ended, tiles = lax.fori_loop(0, N_CTX, finish_block, (empty, empty), unroll=4)
    ended = q_end * ended
    for g in range(4):
        turned = pltpu.roll(ended, (128 - 32 * g) % 128, 1)
        moved = pltpu.roll(tiles, (128 - 8 * g) % 128, 1)
        l_send[g] = jnp.where(lane < 32, turned, moved).astype(BF16)
    send_ctx(5, lambda peer: l_send.at[peer // 8], l_recv)
    l_recv[me] = l_send[me // 8]
    send_ctx(6, lambda peer: m_send.at[peer], m_recv)
    m_recv[me] = m_send[me]

    def turn(received):
        tmp[...] = received[...].reshape(N_CTX * CH, 128).astype(F32).T

    await_bytes(others(e_recv), recv_sem.at[4])
    turn(e_recv)
    ge_recv[rep, ch] = tmp[pl.ds(pl.multiple_of(lax.rem(me, 4) * 32, 32), 32), :].astype(BF16)
    send_ch(7, ge_recv)

    await_bytes(others(l_recv), recv_sem.at[5])
    turn(l_recv)
    four = tmp[pl.ds(pl.multiple_of(my_z // 2 * 8, 8), 8), :]
    gl_recv[rep, ch] = jnp.where(lax.rem(my_z, 2) == 0, four[:4], four[4:])
    send_ch(8, gl_recv)
    scales = tmp[32:40, :]
    m_steps = jnp.sum(jnp.where(iota((8, 512), 0) == my_z, scales, 0.0), axis=0, keepdims=True)

    await_bytes(seven(ge_recv), recv_sem.at[7])
    swap_e = remote(9, ge_recv.at[rep], ge_recv.at[rep], sibling)
    swap_e.start()

    await_bytes(others(m_recv), recv_sem.at[6])
    gain = gain_ref[...]

    def gate(g):
        here = slice(128 * g, 128 * g + 128)
        for h in range(2):
            rows = slice(128 * h, 128 * h + 128)
            codes = decode(m_recv[8 * g : 8 * g + 8, CH * h : CH * h + CH, :]).reshape(128, 128)
            value = codes.T * m_steps[:, here]
            out_ref[rows, here] = (
                query[rows, here] * (value + gain[:, here] * signal[rows, here])
            ).astype(BF16)

    gate(0)
    gate(1)
    await_bytes(seven(gl_recv), recv_sem.at[8])
    swap_l = remote(10, gl_recv.at[rep], gl_recv.at[rep], sibling)
    swap_l.start()
    gate(2)
    gate(3)

    swap_e.wait_recv()
    for c in range(8):
        for r in range(2):
            lanes = slice(512 * (2 * c + r), 512 * (2 * c + r) + 512)
            rows = ge_recv[r, c].astype(F32)
            for k in range(6):
                states_ref[k, :, lanes] = rows[4 * k : 4 * k + 4].astype(BF16)
    swap_l.wait_recv()
    for c in range(8):
        for r in range(2):
            lanes = slice(512 * (2 * c + r), 512 * (2 * c + r) + 512)
            states_ref[6, :, lanes] = gl_recv[r, c].astype(BF16)

    halo_copy.wait_send()
    for n, buffer in ((1, f_recv), (2, r_recv), (3, s_recv), (4, e_recv), (5, l_recv), (6, m_recv)):
        await_bytes(others(buffer), send_sem.at[n])
    await_bytes(seven(ge_recv), send_sem.at[7])
    await_bytes(seven(gl_recv), send_sem.at[8])
    swap_e.wait_send()
    swap_l.wait_send()


def body(projections, short_taps, skip_gain, long_filter, request_ends, replica_of, slot_index):
    first, last, inner, turns = tables()
    whole = pl.BlockSpec(memory_space=pltpu.VMEM)
    operands = (
        projections, long_filter, short_taps, skip_gain.reshape(1, 512),
        request_ends.reshape(1, 128), replica_of.reshape(1, 128), slot_index.reshape(1, 128),
        jnp.asarray(first), jnp.asarray(last), jnp.asarray(inner), jnp.asarray(turns),
    )
    codes = pltpu.VMEM((N_CTX, 2 * CH, 128), jnp.int16)
    tiles = pltpu.VMEM((N_CTX, CH, 128), BF16)
    values = pltpu.VMEM((LEN_A * CH, 128), F32)
    tokens = pltpu.VMEM((TOK, 512), F32)
    output, states = pl.pallas_call(
        kernel,
        out_shape=(
            jax.ShapeDtypeStruct((TOK, 512), BF16),
            jax.ShapeDtypeStruct((7, SLOTS, 8192), BF16),
        ),
        in_specs=[pl.BlockSpec(memory_space=pltpu.HBM)] * len(operands),
        out_specs=(whole, whole),
        scratch_shapes=[
            *[pltpu.VMEM(x.shape, x.dtype) for x in operands],
            pltpu.VMEM((8, 512), F32), pltpu.VMEM((8, 512), F32),
            codes, codes, codes, tiles,
            pltpu.VMEM((8, CH, 128), BF16), pltpu.VMEM((4, CH, 128), BF16),
            codes, codes, codes, tiles, tiles, tiles,
            pltpu.VMEM((2, 8, 32, 512), BF16), pltpu.VMEM((2, 8, SLOTS, 512), F32),
            pltpu.VMEM((64 * CH, 256), F32),
            values, values, values, tokens, tokens,
            pltpu.VMEM((8, 512), F32),
            pltpu.VMEM((128, 1408), BF16),
            pltpu.VMEM((512, 16), F32),
            pltpu.VMEM((128, 512), F32),
            pltpu.SemaphoreType.DMA((11,)),
            pltpu.SemaphoreType.DMA((11,)),
            pltpu.SemaphoreType.DMA((11,)),
        ],
        compiler_params=pltpu.CompilerParams(
            collective_id=0, has_side_effects=True, vmem_limit_bytes=63 * 2**20
        ),
        cost_estimate=pl.CostEstimate(flops=2 * 10**9, bytes_accessed=4 * 10**6, transcendentals=0),
    )(*operands)
    return output, states.transpose(1, 0, 2)


def solution(mesh):
    return jax.shard_map(
        body,
        mesh=mesh,
        in_specs=(
            P(None, "ctx", ("ch", "rep")),
            P(None, None, ("ch", "rep")),
            P(("ch", "rep")),
            P("ctx", ("ch", "rep")),
            P(),
            P(),
            P(),
        ),
        out_specs=(P("ctx", ("ch", "rep")), P("ctx", None, None)),
        check_vma=False,
    )
```

```python
import math

import jax
import jax.numpy as jnp
import ml_dtypes
import numpy as np
from jax import lax
from jax.experimental import pallas as pl
from jax.experimental.pallas import tpu as pltpu
from jax.sharding import PartitionSpec as P

MESH = pl.DeviceIdType.MESH
F32 = jnp.float32
BF16 = jnp.bfloat16

N_CTX = 32
CH = 16
TOK = 256
SEQ = 8192
LEN_A = 64
LEN_B = 128
SLOTS = 4
TOP = 32767.0


def split_np(table):
    high = table.astype(ml_dtypes.bfloat16)
    low = (table - high.astype(np.float64)).astype(ml_dtypes.bfloat16)
    return high, low


def tables():
    k = np.arange(LEN_A) + 0.25
    theta = 2.0 * np.pi * np.outer(k, np.arange(LEN_A)) / LEN_A
    outer = np.concatenate([np.cos(theta), -np.sin(theta)], axis=0)
    o_high, o_low = split_np(outer)
    first = np.concatenate([o_high, o_high, o_low], axis=1)
    e_high, e_low = split_np(outer.T / SEQ)
    last = np.concatenate([e_high, e_low], axis=1)
    phi = 2.0 * np.pi * np.outer(np.arange(LEN_B), np.arange(LEN_B)) / LEN_B
    c, s = np.cos(phi), np.sin(phi)
    inner = np.block([[c, -s], [s, c]])
    i_high, i_low = split_np(inner)
    v_high, v_low = split_np(inner.T)
    inner_all = np.stack([i_high, i_low, v_high, v_low])
    turn = 2.0 * np.pi * np.outer(k, np.arange(LEN_B)) / SEQ
    turns = np.stack([np.tile(np.cos(turn), (1, 2)), np.tile(np.sin(turn), (1, 2))]).astype(np.float32)
    return first, last, inner_all, turns


def row_scale(block, axis):
    largest = jnp.max(jnp.abs(block), axis=axis, keepdims=True)
    step = jnp.maximum(largest, 2.0**-100) * (1.0078125 / TOP)
    return step.astype(BF16).astype(F32)


def code(scaled):
    return jnp.floor(scaled + 0.5).astype(jnp.int32).astype(jnp.int16)


def decode(codes):
    return codes.astype(jnp.int32).astype(F32)


def iota(shape, axis):
    return lax.broadcasted_iota(jnp.int32, shape, axis)


def split(value):
    high = value.astype(BF16)
    return high, (value - high.astype(F32)).astype(BF16)


def dot(a, b):
    return jnp.dot(a, b, preferred_element_type=F32)


def kernel(*refs):
    hbm_refs, (out_ref, states_ref), vmem_refs = refs[:11], refs[11:13], refs[13:24]
    (
        proj, filt, taps_ref, gain_ref, ends_ref, repl_ref, slot_ref,
        first_ref, last_ref, inner_ref, turns_ref,
    ) = vmem_refs
    (
        halo_send, halo_recv, step_send, step_recv, f_send, s_send, m_send, r_send, e_send, l_send,
        f_recv, s_recv, m_recv, r_recv, e_recv, l_recv, ge_recv, gl_recv,
        spec, filter_t, sig_t, mixed, query, signal, steps, onehot, taps_t, tmp,
        local_sem, send_sem, recv_sem,
    ) = refs[24:]
    me = lax.axis_index("ctx")
    ch, rep = lax.axis_index("ch"), lax.axis_index("rep")
    my_x, my_z = me // 8, lax.rem(me, 8)
    after = {"ctx": lax.rem(me + 1, N_CTX)}
    sibling = {"rep": 1 - rep}

    loads = [
        pltpu.make_async_copy(source, target, local_sem.at[n])
        for n, (source, target) in enumerate(zip(hbm_refs, vmem_refs))
    ]
    for load in loads:
        load.start()

    barrier = pltpu.get_barrier_semaphore()

    def greet(device):
        pl.semaphore_signal(barrier, inc=1, device_id=device, device_id_type=MESH)

    def greet_ctx(t, carry):
        greet({"ctx": lax.rem(me + t, N_CTX)})
        return carry

    mine_near = ch * 2 + rep

    def near(t):
        other = lax.rem(mine_near + t, 16)
        return {"ch": other // 2, "rep": lax.rem(other, 2)}

    def greet_near(t, carry):
        greet(near(t))
        return carry

    lax.fori_loop(1, N_CTX, greet_ctx, 0)
    lax.fori_loop(1, 16, greet_near, 0)

    def remote(n, source, target, device):
        return pltpu.make_async_remote_copy(
            src_ref=source, dst_ref=target,
            send_sem=send_sem.at[n], recv_sem=recv_sem.at[n],
            device_id=device, device_id_type=MESH,
        )

    def send_line(n, source, target, dx):
        x = lax.rem(my_x + dx, 4)

        def one(t, carry):
            peer = 8 * x + lax.rem(my_z + t, 8)
            remote(n, source(peer), target.at[me], {"ctx": peer}).start()
            return carry

        lax.fori_loop(1 if dx == 0 else 0, 8, one, 0)

    def send_ctx(n, source, target):
        for dx in range(4):
            send_line(n, source, target, dx)

    def send_ch(n, buffer):
        def one(t, carry):
            remote(n, buffer.at[rep, ch], buffer.at[rep, ch], {"ch": lax.rem(ch + t, 8)}).start()
            return carry

        lax.fori_loop(1, 8, one, 0)

    def send_near(n, buffer):
        def one(t, carry):
            remote(n, buffer.at[mine_near], buffer.at[mine_near], near(t)).start()
            return carry

        lax.fori_loop(1, 16, one, 0)

    def await_bytes(part, sem):
        pltpu.make_async_copy(part, part, sem).wait()

    def others(buffer):
        return buffer.at[pl.ds(0, N_CTX - 1)]

    def seven(buffer):
        return buffer.at[0, pl.ds(0, 7)]

    def column_block(dx):
        g = lax.rem(my_x + dx, 4)
        return pl.ds(pl.multiple_of(8 * g, 8), 8), pl.ds(pl.multiple_of(128 * g, 128), 128)

    def put_codes(block, kind, dx, target):
        devices, lanes = column_block(dx)
        step = row_scale(block, 0)
        steps[kind : kind + 1, lanes] = step
        turned = (block * (1.0 / step)).T.reshape(8, CH, TOK)
        parts = [
            turned[:, 8 * q : 8 * q + 8, 128 * h : 128 * h + 128] for q in range(2) for h in range(2)
        ]
        target[devices] = code(jnp.concatenate(parts, axis=1))

    def put_filter(dx):
        lanes = column_block(dx)[1]
        put_codes(filt[:, lanes], 0, dx, f_send)
        step_send[lax.rem(my_x + dx, 4)] = steps[0:1, lanes]

    loads[0].wait()
    halo_send[...] = jnp.concatenate(
        [proj[p, TOK - 16 :, :].astype(F32)[14:] for p in range(3)] + [jnp.zeros((2, 512), F32)], axis=0
    )
    steps[...] = jnp.zeros((8, 512), F32)
    loads[1].wait()
    put_filter(0)
    pl.semaphore_wait(barrier, N_CTX - 1 + 15)
    halo_copy = remote(0, halo_send, halo_recv, after)
    halo_copy.start()
    for dx in range(4):
        if dx > 0:
            put_filter(dx)
        send_line(1, lambda peer: f_send.at[peer], f_recv, dx)
        send_line(9, lambda peer: step_send.at[peer // 8], step_recv, dx)
    f_recv[me] = f_send[me]
    step_recv[me] = step_send[me // 8]
    for load in loads[2:]:
        load.wait()

    ends = ends_ref[...]
    end_block = ends // TOK
    end_lane = ends - end_block * TOK

    def down(row):
        return jnp.broadcast_to(row, (128, 128)).T

    earlier = iota((128, 128), 0) < iota((128, 128), 1)
    same = down(end_block) == end_block
    rank = jnp.sum(jnp.where(earlier, jnp.where(same, 1, 0), 0), axis=0, keepdims=True)
    slot_of = down(repl_ref[...] * SLOTS + slot_ref[...])

    def at_slot(row, slots):
        values = down(row)[:, :1]
        hit = slot_of[:, :1] == slots
        return jnp.sum(jnp.where(hit, values, 0), axis=0, keepdims=True)

    where_code = end_block * 16 + rank
    column = iota((128, 1024), 1)
    e_code = at_slot(where_code, column // 32 * 4 + column % 4)
    slots_row = iota((128, 128), 1)
    t_code = at_slot(where_code, slots_row)
    t_end = at_slot(ends, slots_row)
    row_kind = iota((1, 1024), 1) % 32 // 4
    code_all = jnp.concatenate([e_code, t_code, t_code, t_code], axis=1)
    kind_all = jnp.concatenate(
        [jnp.where(row_kind < 6, row_kind + 1, -10)] + [jnp.full((1, 128), k, jnp.int32) for k in range(3)],
        axis=1,
    )
    block_all = code_all // 16
    lane_all = kind_all * 16 + (code_all - block_all * 16)
    onehot[...] = jnp.where(iota((128, 1408), 0) == lane_all, 1.0, 0.0).astype(BF16)

    mine = jnp.where(end_block == me, jnp.where(rank == iota((16, 128), 0), end_lane + 100, 0), 0)
    place = jnp.sum(mine, axis=1, keepdims=True) - 100
    token = iota((16, TOK), 1)

    def rows_at(back):
        return jnp.where(token == place - back, 1.0, 0.0).astype(BF16)

    two_rows = jnp.concatenate([rows_at(1), rows_at(0)], axis=0)
    three_rows = jnp.concatenate([rows_at(2), two_rows], axis=0)

    halo_copy.wait_recv()
    token_row = iota((TOK, 128), 0)
    for dx in range(4):
        devices, lanes = column_block(dx)
        conv = []
        halo_here = jnp.where(me > 0, halo_recv[:, lanes], 0.0)
        for p in range(3):
            x = proj[p, :, lanes].astype(F32)
            tail2, tail1 = halo_here[2 * p : 2 * p + 1], halo_here[2 * p + 1 : 2 * p + 2]
            back1 = jnp.where(token_row < 1, tail1, pltpu.roll(x, 1, 0))
            back2 = jnp.where(
                token_row < 1, tail2, jnp.where(token_row < 2, tail1, pltpu.roll(x, 2, 0))
            )
            taps = taps_ref[p, :, lanes]
            conv.append(taps[0:1] * x + taps[1:2] * back1 + taps[2:3] * back2)
        query[:, lanes] = conv[0]
        product = conv[1] * conv[2]
        signal[:, lanes] = product
        put_codes(product, 1, dx, s_send)
        q_rows = dot(three_rows, proj[0, :, lanes])
        first_rows = q_rows[:16] + jnp.where(place == 1, halo_here[1:2], 0.0)
        rows = jnp.concatenate(
            [
                first_rows, q_rows[16:], dot(two_rows, proj[1, :, lanes]), dot(two_rows, proj[2, :, lanes]),
                steps[:, lanes], jnp.zeros((8, 128), F32),
            ],
            axis=0,
        )
        r_send[devices] = rows.T.astype(BF16).reshape(8, CH, 128)
        send_line(2, lambda peer: r_send.at[peer], r_recv, dx)
    r_recv[me] = r_send[me]
    half = [pl.ds(CH * q, CH) for q in range(2)]

    def send_half(n, q, source, target):
        for dx in range(4):
            x = lax.rem(my_x + dx, 4)

            def one(t, carry):
                peer = 8 * x + lax.rem(my_z + t, 8)
                remote(n, source.at[peer, half[q]], target.at[me, half[q]], {"ctx": peer}).start()
                return carry

            lax.fori_loop(1 if dx == 0 else 0, 8, one, 0)

    send_half(3, 0, s_send, s_recv)
    send_half(10, 1, s_send, s_recv)
    s_recv[me] = s_send[me]

    rows = [taps_ref[p] for p in range(3)] + [gain_ref[...], jnp.zeros((6, 512), F32)]
    taps_t[...] = jnp.concatenate(rows, axis=0).T
    my_taps = taps_t[pl.ds(pl.multiple_of(me * CH, CH), CH), :]

    cos_t, sin_t = turns_ref[0], turns_ref[1]

    def read_codes(received, q, step_of, target):
        for i in range(N_CTX):
            step = step_of(i)[8 * q : 8 * q + 8]
            step = jnp.concatenate([step, step], axis=0)
            target[q, 16 * i : 16 * i + 16, :] = decode(received[i, CH * q : CH * q + CH, :]) * step

    def forward(ref):
        turned = []
        for c in range(0, 8, 2):
            x = jnp.concatenate([ref[pl.ds(c + n, LEN_A, stride=8), :] for n in range(2)], axis=1)
            high, low = split(x)
            z = dot(first_ref[...], jnp.concatenate([high, low, high], axis=0))
            re, im = z[:64], z[64:]
            zr = re * cos_t + im * sin_t
            zi = im * cos_t - re * sin_t
            for n in (slice(0, 128), slice(128, 256)):
                turned.append(jnp.concatenate([zr[:, n], zi[:, n]], axis=1))
        high, low = split(jnp.concatenate(turned, axis=0))
        return dot(high, inner_ref[0]) + (dot(low, inner_ref[0]) + dot(high, inner_ref[1]))

    await_bytes(others(f_recv), recv_sem.at[1])
    await_bytes(others(step_recv), recv_sem.at[9])
    tmp[:, :32] = step_recv[...].reshape(N_CTX, 128).T
    f_steps = tmp[pl.ds(pl.multiple_of(my_z * CH, CH), CH), :32]
    for q in range(2):
        read_codes(f_recv, q, lambda i: f_steps[:, i : i + 1], filter_t)
        spec[q] = forward(filter_t.at[q])

    await_bytes(others(r_recv), recv_sem.at[2])
    def gather_four(i, total):
        blocks = r_recv[pl.ds(pl.multiple_of(4 * i, 4), 4)].reshape(4 * CH, 128)
        found = dot(blocks, onehot[...])
        for u in range(4):
            total = total + jnp.where(block_all == 4 * i + u, found[CH * u : CH * u + CH], 0.0)
        return total

    wanted = lax.fori_loop(0, N_CTX // 4, gather_four, jnp.zeros((CH, 1408), F32))
    for g in range(8):
        e_send[g] = wanted[:, 128 * g : 128 * g + 128].astype(BF16)
    send_ctx(4, lambda peer: e_send.at[peer // 4], e_recv)
    e_recv[me] = e_send[me // 4]
    q_end = (
        my_taps[:, 2:3] * wanted[:, 1024:1152]
        + my_taps[:, 1:2] * wanted[:, 1152:1280]
        + my_taps[:, 0:1] * wanted[:, 1280:1408]
    )

    lane = iota((8, 128), 1)
    end_half = t_end // 128
    end_spot = t_end - end_half * 128
    spot = jnp.where(iota((128, 128), 0) == end_spot, 1.0, 0.0).astype(BF16)
    spots = jnp.concatenate([spot, spot], axis=0)

    def convolve(q):
        read_codes(s_recv, q, lambda i: r_recv[i].astype(F32)[:, 113:114], sig_t)
        x, f = forward(sig_t.at[q]), spec[q]
        xr, xi, fr, fi = x[:, :128], x[:, 128:], f[:, :128], f[:, 128:]
        y = jnp.concatenate([xr * fr - xi * fi, xr * fi + xi * fr], axis=1)
        high, low = split(y)
        u = dot(high, inner_ref[2]) + (dot(low, inner_ref[2]) + dot(high, inner_ref[3]))
        for c in range(0, 8, 2):
            one, two = u[64 * c : 64 * c + 64], u[64 * c + 64 : 64 * c + 128]
            ur = jnp.concatenate([one[:, :128], two[:, :128]], axis=1)
            ui = jnp.concatenate([one[:, 128:], two[:, 128:]], axis=1)
            w = jnp.concatenate([ur * cos_t - ui * sin_t, ui * cos_t + ur * sin_t], axis=0)
            high, low = split(w)
            y = dot(last_ref[...], jnp.concatenate([high, high], axis=0)) + dot(last_ref[:, :128], low)
            mixed[pl.ds(c, LEN_A, stride=8), :] = y[:, :128]
            mixed[pl.ds(c + 1, LEN_A, stride=8), :] = y[:, 128:]

    def put_mixed(q):
        gain_col = my_taps[8 * q : 8 * q + 8, 9:10]
        gain_col = jnp.concatenate([gain_col] * 8, axis=0)

        def four_blocks(j, carry):
            ended, tiles = carry
            here = pl.ds(pl.multiple_of(j * 64, 64), 64)
            y = mixed[here, :]
            high, low = split(y + gain_col * sig_t[q, here, :])
            found = dot(jnp.concatenate([high, low], axis=1), spots)
            for u in range(8):
                ended = ended + jnp.where(end_half == 8 * j + u, found[8 * u : 8 * u + 8], 0.0)
            for u in range(4):
                block = y[16 * u : 16 * u + 16]
                step = row_scale(jnp.maximum(jnp.abs(block[:8]), jnp.abs(block[8:])), 1)
                both = jnp.concatenate([step, step], axis=0)
                m_send[4 * j + u, CH * q : CH * q + CH] = code(block * (1.0 / both))
                tiles = jnp.where(lane == 32 + 4 * j + u, step, tiles)
            return ended, tiles

        empty = jnp.zeros((8, 128), F32)
        return lax.fori_loop(0, N_CTX // 4, four_blocks, (empty, empty), unroll=2)

    def turn(received):
        tmp[...] = received[...].reshape(N_CTX * CH, 128).astype(F32).T

    await_bytes(s_recv.at[pl.ds(0, N_CTX - 1), half[0]], recv_sem.at[3])
    convolve(0)
    ended0, tiles0 = put_mixed(0)
    send_half(6, 0, m_send, m_recv)

    await_bytes(s_recv.at[pl.ds(0, N_CTX - 1), half[1]], recv_sem.at[10])
    convolve(1)
    ended1, tiles1 = put_mixed(1)
    ended = q_end * jnp.concatenate([ended0, ended1], axis=0)
    tiles = jnp.concatenate([tiles0, tiles1], axis=0)
    lane = iota((CH, 128), 1)
    for g in range(4):
        turned = pltpu.roll(ended, (128 - 32 * g) % 128, 1)
        moved = pltpu.roll(tiles, (128 - 8 * g) % 128, 1)
        l_send[g] = jnp.where(lane < 32, turned, moved).astype(BF16)
    send_ctx(5, lambda peer: l_send.at[peer // 8], l_recv)
    l_recv[me] = l_send[me // 8]

    await_bytes(others(e_recv), recv_sem.at[4])
    turn(e_recv)
    ge_recv[rep, ch] = tmp[pl.ds(pl.multiple_of(lax.rem(me, 4) * 32, 32), 32), :].astype(BF16)
    send_ch(7, ge_recv)

    send_half(11, 1, m_send, m_recv)
    m_recv[me] = m_send[me]

    await_bytes(seven(ge_recv), recv_sem.at[7])
    swap_e = remote(12, ge_recv.at[rep], ge_recv.at[rep], sibling)
    swap_e.start()

    await_bytes(others(l_recv), recv_sem.at[5])
    turn(l_recv)
    four = tmp[pl.ds(pl.multiple_of(my_z // 2 * 8, 8), 8), :]
    gl_recv[mine_near] = jnp.where(lax.rem(my_z, 2) == 0, four[:4], four[4:])
    send_near(8, gl_recv)
    scales = tmp[32:40, :]
    m_steps = jnp.sum(jnp.where(iota((8, 512), 0) == my_z, scales, 0.0), axis=0, keepdims=True)

    await_bytes(m_recv.at[pl.ds(0, N_CTX - 1), half[0]], recv_sem.at[6])
    await_bytes(m_recv.at[pl.ds(0, N_CTX - 1), half[1]], recv_sem.at[11])
    gain = gain_ref[...]

    for g in range(4):
        here = slice(128 * g, 128 * g + 128)
        codes = decode(m_recv[8 * g : 8 * g + 8])
        for h in range(2):
            rows = slice(128 * h, 128 * h + 128)
            parts = [codes[:, CH * q + 8 * h : CH * q + 8 * h + 8] for q in range(2)]
            value = jnp.concatenate(parts, axis=1).reshape(128, 128).T * m_steps[:, here]
            out_ref[rows, here] = (
                query[rows, here] * (value + gain[:, here] * signal[rows, here])
            ).astype(BF16)

    swap_e.wait_recv()
    for c in range(8):
        for r in range(2):
            lanes = slice(512 * (2 * c + r), 512 * (2 * c + r) + 512)
            rows = ge_recv[r, c].astype(F32)
            for k in range(6):
                states_ref[k, :, lanes] = rows[4 * k : 4 * k + 4].astype(BF16)
    await_bytes(gl_recv.at[pl.ds(0, 15)], recv_sem.at[8])
    for j in range(16):
        states_ref[6, :, 512 * j : 512 * j + 512] = gl_recv[j].astype(BF16)

    halo_copy.wait_send()
    for n, buffer in ((1, f_recv), (2, r_recv), (4, e_recv), (5, l_recv), (9, step_recv)):
        await_bytes(others(buffer), send_sem.at[n])
    for n, buffer in ((3, s_recv), (6, m_recv), (10, s_recv), (11, m_recv)):
        await_bytes(buffer.at[pl.ds(0, N_CTX - 1), half[0]], send_sem.at[n])
    await_bytes(seven(ge_recv), send_sem.at[7])
    await_bytes(gl_recv.at[pl.ds(0, 15)], send_sem.at[8])
    swap_e.wait_send()


def body(projections, short_taps, skip_gain, long_filter, request_ends, replica_of, slot_index):
    first, last, inner, turns = tables()
    whole = pl.BlockSpec(memory_space=pltpu.VMEM)
    operands = (
        projections, long_filter, short_taps, skip_gain.reshape(1, 512),
        request_ends.reshape(1, 128), replica_of.reshape(1, 128), slot_index.reshape(1, 128),
        jnp.asarray(first), jnp.asarray(last), jnp.asarray(inner), jnp.asarray(turns),
    )
    codes = pltpu.VMEM((N_CTX, 2 * CH, 128), jnp.int16)
    tiles = pltpu.VMEM((N_CTX, CH, 128), BF16)
    values = pltpu.VMEM((2, 512, 128), F32)
    tokens = pltpu.VMEM((TOK, 512), F32)
    output, states = pl.pallas_call(
        kernel,
        out_shape=(
            jax.ShapeDtypeStruct((TOK, 512), BF16),
            jax.ShapeDtypeStruct((7, SLOTS, 8192), BF16),
        ),
        in_specs=[pl.BlockSpec(memory_space=pltpu.HBM)] * len(operands),
        out_specs=(whole, whole),
        scratch_shapes=[
            *[pltpu.VMEM(x.shape, x.dtype) for x in operands],
            pltpu.VMEM((8, 512), F32), pltpu.VMEM((8, 512), F32),
            pltpu.VMEM((4, 1, 128), F32), pltpu.VMEM((N_CTX, 1, 128), F32),
            codes, codes, codes, tiles,
            pltpu.VMEM((8, CH, 128), BF16), pltpu.VMEM((4, CH, 128), BF16),
            codes, codes, codes, tiles, tiles, tiles,
            pltpu.VMEM((2, 8, 32, 512), BF16), pltpu.VMEM((16, SLOTS, 512), F32),
            pltpu.VMEM((2, 512, 256), F32),
            values, values, pltpu.VMEM((512, 128), F32), tokens, tokens,
            pltpu.VMEM((8, 512), F32),
            pltpu.VMEM((128, 1408), BF16),
            pltpu.VMEM((512, 16), F32),
            pltpu.VMEM((128, 512), F32),
            pltpu.SemaphoreType.DMA((11,)),
            pltpu.SemaphoreType.DMA((13,)),
            pltpu.SemaphoreType.DMA((13,)),
        ],
        compiler_params=pltpu.CompilerParams(
            collective_id=0, has_side_effects=True, vmem_limit_bytes=63 * 2**20
        ),
        cost_estimate=pl.CostEstimate(flops=2 * 10**9, bytes_accessed=4 * 10**6, transcendentals=0),
    )(*operands)
    return output, states.transpose(1, 0, 2)


def solution(mesh):
    return jax.shard_map(
        body,
        mesh=mesh,
        in_specs=(
            P(None, "ctx", ("ch", "rep")),
            P(None, None, ("ch", "rep")),
            P(("ch", "rep")),
            P("ctx", ("ch", "rep")),
            P(),
            P(),
            P(),
        ),
        out_specs=(P("ctx", ("ch", "rep")), P("ctx", None, None)),
        check_vma=False,
    )
```

```python
import math

import jax
import jax.numpy as jnp
import ml_dtypes
import numpy as np
from jax import lax
from jax.experimental import pallas as pl
from jax.experimental.pallas import tpu as pltpu
from jax.sharding import PartitionSpec as P

MESH = pl.DeviceIdType.MESH
F32 = jnp.float32
BF16 = jnp.bfloat16

N_CTX = 32
CH = 16
TOK = 256
SEQ = 8192
LEN_A = 64
LEN_B = 128
SLOTS = 4
TOP = 32767.0


def split_np(table):
    high = table.astype(ml_dtypes.bfloat16)
    low = (table - high.astype(np.float64)).astype(ml_dtypes.bfloat16)
    return high, low


def tables():
    k = np.arange(LEN_A) + 0.25
    theta = 2.0 * np.pi * np.outer(k, np.arange(LEN_A)) / LEN_A
    outer = np.concatenate([np.cos(theta), -np.sin(theta)], axis=0)
    o_high, o_low = split_np(outer)
    first = np.concatenate([o_high, o_high, o_low], axis=1)
    e_high, e_low = split_np(outer.T / SEQ)
    last = np.concatenate([e_high, e_low], axis=1)
    phi = 2.0 * np.pi * np.outer(np.arange(LEN_B), np.arange(LEN_B)) / LEN_B
    c, s = np.cos(phi), np.sin(phi)
    inner = np.block([[c, -s], [s, c]])
    i_high, i_low = split_np(inner)
    v_high, v_low = split_np(inner.T)
    inner_all = np.stack([i_high, i_low, v_high, v_low])
    turn = 2.0 * np.pi * np.outer(k, np.arange(LEN_B)) / SEQ
    turns = np.stack([np.tile(np.cos(turn), (1, 2)), np.tile(np.sin(turn), (1, 2))]).astype(np.float32)
    return first, last, inner_all, turns


def row_scale(block, axis):
    largest = jnp.max(jnp.abs(block), axis=axis, keepdims=True)
    step = jnp.maximum(largest, 2.0**-100) * (1.0078125 / TOP)
    return step.astype(BF16).astype(F32)


def code(scaled):
    return jnp.floor(scaled + 0.5).astype(jnp.int32).astype(jnp.int16)


def decode(codes):
    return codes.astype(jnp.int32).astype(F32)


def iota(shape, axis):
    return lax.broadcasted_iota(jnp.int32, shape, axis)


def split(value):
    high = value.astype(BF16)
    return high, (value - high.astype(F32)).astype(BF16)


def dot(a, b):
    return jnp.dot(a, b, preferred_element_type=F32)


def kernel(*refs):
    hbm_refs, (out_ref, states_ref), vmem_refs = refs[:11], refs[11:13], refs[13:24]
    (
        proj, filt, taps_ref, gain_ref, ends_ref, repl_ref, slot_ref,
        first_ref, last_ref, inner_ref, turns_ref,
    ) = vmem_refs
    (
        halo_send, halo_recv, step_send, step_recv, f_send, s_send, m_send, r_send, e_send, l_send,
        f_recv, s_recv, m_recv, r_recv, e_recv, l_recv, ge_recv, gl_recv,
        spec, filter_t, sig_t, mixed, query, signal, steps, onehot, taps_t, tmp,
        local_sem, send_sem, recv_sem,
    ) = refs[24:]
    me = lax.axis_index("ctx")
    ch, rep = lax.axis_index("ch"), lax.axis_index("rep")
    my_x, my_z = me // 8, lax.rem(me, 8)
    after = {"ctx": lax.rem(me + 1, N_CTX)}
    sibling = {"rep": 1 - rep}

    loads = [
        pltpu.make_async_copy(source, target, local_sem.at[n])
        for n, (source, target) in enumerate(zip(hbm_refs, vmem_refs))
    ]
    for load in loads:
        load.start()

    barrier = pltpu.get_barrier_semaphore()

    def greet(device):
        pl.semaphore_signal(barrier, inc=1, device_id=device, device_id_type=MESH)

    def greet_ctx(t, carry):
        greet({"ctx": lax.rem(me + t, N_CTX)})
        return carry

    mine_near = ch * 2 + rep

    def near(t):
        other = lax.rem(mine_near + t, 16)
        return {"ch": other // 2, "rep": lax.rem(other, 2)}

    def greet_near(t, carry):
        greet(near(t))
        return carry

    lax.fori_loop(1, N_CTX, greet_ctx, 0)
    lax.fori_loop(1, 16, greet_near, 0)

    def remote(n, source, target, device):
        return pltpu.make_async_remote_copy(
            src_ref=source, dst_ref=target,
            send_sem=send_sem.at[n], recv_sem=recv_sem.at[n],
            device_id=device, device_id_type=MESH,
        )

    def send_line(n, source, target, dx):
        x = lax.rem(my_x + dx, 4)

        def one(t, carry):
            peer = 8 * x + lax.rem(my_z + t, 8)
            remote(n, source(peer), target.at[me], {"ctx": peer}).start()
            return carry

        lax.fori_loop(1 if dx == 0 else 0, 8, one, 0)

    def send_ctx(n, source, target):
        for dx in range(4):
            send_line(n, source, target, dx)

    def send_ch(n, buffer):
        def one(t, carry):
            remote(n, buffer.at[rep, ch], buffer.at[rep, ch], {"ch": lax.rem(ch + t, 8)}).start()
            return carry

        lax.fori_loop(1, 8, one, 0)

    def send_near(n, buffer):
        def one(t, carry):
            remote(n, buffer.at[mine_near], buffer.at[mine_near], near(t)).start()
            return carry

        lax.fori_loop(1, 16, one, 0)

    def await_bytes(part, sem):
        pltpu.make_async_copy(part, part, sem).wait()

    def others(buffer):
        return buffer.at[pl.ds(0, N_CTX - 1)]

    def seven(buffer):
        return buffer.at[0, pl.ds(0, 7)]

    def column_block(dx):
        g = lax.rem(my_x + dx, 4)
        return pl.ds(pl.multiple_of(8 * g, 8), 8), pl.ds(pl.multiple_of(128 * g, 128), 128)

    def put_codes(block, kind, dx, target):
        devices, lanes = column_block(dx)
        step = row_scale(block, 0)
        steps[kind : kind + 1, lanes] = step
        turned = (block * (1.0 / step)).T.reshape(8, CH, TOK)
        parts = [
            turned[:, 8 * q : 8 * q + 8, 128 * h : 128 * h + 128] for q in range(2) for h in range(2)
        ]
        target[devices] = code(jnp.concatenate(parts, axis=1))

    def put_filter(dx):
        lanes = column_block(dx)[1]
        put_codes(filt[:, lanes], 0, dx, f_send)
        step_send[lax.rem(my_x + dx, 4)] = steps[0:1, lanes]

    loads[0].wait()
    halo_send[...] = jnp.concatenate(
        [proj[p, TOK - 16 :, :].astype(F32)[14:] for p in range(3)] + [jnp.zeros((2, 512), F32)], axis=0
    )
    steps[...] = jnp.zeros((8, 512), F32)
    loads[1].wait()
    put_filter(0)
    pl.semaphore_wait(barrier, N_CTX - 1 + 15)
    halo_copy = remote(0, halo_send, halo_recv, after)
    halo_copy.start()
    for dx in range(4):
        if dx > 0:
            put_filter(dx)
        send_line(1, lambda peer: f_send.at[peer], f_recv, dx)
        send_line(9, lambda peer: step_send.at[peer // 8], step_recv, dx)
    f_recv[me] = f_send[me]
    step_recv[me] = step_send[me // 8]
    for load in loads[2:]:
        load.wait()

    ends = ends_ref[...]
    end_block = ends // TOK
    end_lane = ends - end_block * TOK

    def down(row):
        return jnp.broadcast_to(row, (128, 128)).T

    earlier = iota((128, 128), 0) < iota((128, 128), 1)
    same = down(end_block) == end_block
    rank = jnp.sum(jnp.where(earlier, jnp.where(same, 1, 0), 0), axis=0, keepdims=True)
    slot_of = down(repl_ref[...] * SLOTS + slot_ref[...])

    def at_slot(row, slots):
        values = down(row)[:, :1]
        hit = slot_of[:, :1] == slots
        return jnp.sum(jnp.where(hit, values, 0), axis=0, keepdims=True)

    where_code = end_block * 16 + rank
    column = iota((128, 1024), 1)
    e_code = at_slot(where_code, column // 32 * 4 + column % 4)
    slots_row = iota((128, 128), 1)
    t_code = at_slot(where_code, slots_row)
    t_end = at_slot(ends, slots_row)
    row_kind = iota((1, 1024), 1) % 32 // 4
    code_all = jnp.concatenate([e_code, t_code, t_code, t_code], axis=1)
    kind_all = jnp.concatenate(
        [jnp.where(row_kind < 6, row_kind + 1, -10)] + [jnp.full((1, 128), k, jnp.int32) for k in range(3)],
        axis=1,
    )
    block_all = code_all // 16
    lane_all = kind_all * 16 + (code_all - block_all * 16)
    onehot[...] = jnp.where(iota((128, 1408), 0) == lane_all, 1.0, 0.0).astype(BF16)

    mine = jnp.where(end_block == me, jnp.where(rank == iota((16, 128), 0), end_lane + 100, 0), 0)
    place = jnp.sum(mine, axis=1, keepdims=True) - 100
    token = iota((16, TOK), 1)

    def rows_at(back):
        return jnp.where(token == place - back, 1.0, 0.0).astype(BF16)

    two_rows = jnp.concatenate([rows_at(1), rows_at(0)], axis=0)
    three_rows = jnp.concatenate([rows_at(2), two_rows], axis=0)

    halo_copy.wait_recv()
    token_row = iota((TOK, 128), 0)
    for dx in range(4):
        devices, lanes = column_block(dx)
        conv = []
        halo_here = jnp.where(me > 0, halo_recv[:, lanes], 0.0)
        for p in range(3):
            x = proj[p, :, lanes].astype(F32)
            tail2, tail1 = halo_here[2 * p : 2 * p + 1], halo_here[2 * p + 1 : 2 * p + 2]
            back1 = jnp.where(token_row < 1, tail1, pltpu.roll(x, 1, 0))
            back2 = jnp.where(
                token_row < 1, tail2, jnp.where(token_row < 2, tail1, pltpu.roll(x, 2, 0))
            )
            taps = taps_ref[p, :, lanes]
            conv.append(taps[0:1] * x + taps[1:2] * back1 + taps[2:3] * back2)
        query[:, lanes] = conv[0]
        product = conv[1] * conv[2]
        signal[:, lanes] = product
        put_codes(product, 1, dx, s_send)
        q_rows = dot(three_rows, proj[0, :, lanes])
        first_rows = q_rows[:16] + jnp.where(place == 1, halo_here[1:2], 0.0)
        rows = jnp.concatenate(
            [
                first_rows, q_rows[16:], dot(two_rows, proj[1, :, lanes]), dot(two_rows, proj[2, :, lanes]),
                steps[:, lanes], jnp.zeros((8, 128), F32),
            ],
            axis=0,
        )
        r_send[devices] = rows.T.astype(BF16).reshape(8, CH, 128)
        send_line(2, lambda peer: r_send.at[peer], r_recv, dx)
    r_recv[me] = r_send[me]
    half = [pl.ds(CH * q, CH) for q in range(2)]

    def send_half(n, q, source, target):
        for dx in range(4):
            x = lax.rem(my_x + dx, 4)

            def one(t, carry):
                peer = 8 * x + lax.rem(my_z + t, 8)
                remote(n, source.at[peer, half[q]], target.at[me, half[q]], {"ctx": peer}).start()
                return carry

            lax.fori_loop(1 if dx == 0 else 0, 8, one, 0)

    send_half(3, 0, s_send, s_recv)
    send_half(10, 1, s_send, s_recv)
    s_recv[me] = s_send[me]

    rows = [taps_ref[p] for p in range(3)] + [gain_ref[...], jnp.zeros((6, 512), F32)]
    taps_t[...] = jnp.concatenate(rows, axis=0).T
    my_taps = taps_t[pl.ds(pl.multiple_of(me * CH, CH), CH), :]

    cos_t, sin_t = turns_ref[0], turns_ref[1]

    def read_codes(received, q, step_of, target):
        for i in range(N_CTX):
            step = step_of(i)[8 * q : 8 * q + 8]
            step = jnp.concatenate([step, step], axis=0)
            target[q, 16 * i : 16 * i + 16, :] = decode(received[i, CH * q : CH * q + CH, :]) * step

    def forward(ref):
        turned = []
        for c in range(0, 8, 2):
            x = jnp.concatenate([ref[pl.ds(c + n, LEN_A, stride=8), :] for n in range(2)], axis=1)
            high, low = split(x)
            z = dot(first_ref[...], jnp.concatenate([high, low, high], axis=0))
            re, im = z[:64], z[64:]
            zr = re * cos_t + im * sin_t
            zi = im * cos_t - re * sin_t
            for n in (slice(0, 128), slice(128, 256)):
                turned.append(jnp.concatenate([zr[:, n], zi[:, n]], axis=1))
        high, low = split(jnp.concatenate(turned, axis=0))
        return dot(high, inner_ref[0]) + (dot(low, inner_ref[0]) + dot(high, inner_ref[1]))

    await_bytes(others(f_recv), recv_sem.at[1])
    await_bytes(others(step_recv), recv_sem.at[9])
    tmp[:, :32] = step_recv[...].reshape(N_CTX, 128).T
    f_steps = tmp[pl.ds(pl.multiple_of(my_z * CH, CH), CH), :32]
    for q in range(2):
        read_codes(f_recv, q, lambda i: f_steps[:, i : i + 1], filter_t)
        spec[q] = forward(filter_t.at[q])

    await_bytes(others(r_recv), recv_sem.at[2])
    def gather_four(i, total):
        blocks = r_recv[pl.ds(pl.multiple_of(4 * i, 4), 4)].reshape(4 * CH, 128)
        found = dot(blocks, onehot[...])
        for u in range(4):
            total = total + jnp.where(block_all == 4 * i + u, found[CH * u : CH * u + CH], 0.0)
        return total

    wanted = lax.fori_loop(0, N_CTX // 4, gather_four, jnp.zeros((CH, 1408), F32))
    for g in range(8):
        e_send[g] = wanted[:, 128 * g : 128 * g + 128].astype(BF16)
    send_ctx(4, lambda peer: e_send.at[peer // 4], e_recv)
    e_recv[me] = e_send[me // 4]
    q_end = (
        my_taps[:, 2:3] * wanted[:, 1024:1152]
        + my_taps[:, 1:2] * wanted[:, 1152:1280]
        + my_taps[:, 0:1] * wanted[:, 1280:1408]
    )

    lane = iota((8, 128), 1)
    end_half = t_end // 128
    end_spot = t_end - end_half * 128
    spot = jnp.where(iota((128, 128), 0) == end_spot, 1.0, 0.0).astype(BF16)
    spots = jnp.concatenate([spot, spot], axis=0)

    def convolve(q):
        read_codes(s_recv, q, lambda i: r_recv[i].astype(F32)[:, 113:114], sig_t)
        x, f = forward(sig_t.at[q]), spec[q]
        xr, xi, fr, fi = x[:, :128], x[:, 128:], f[:, :128], f[:, 128:]
        y = jnp.concatenate([xr * fr - xi * fi, xr * fi + xi * fr], axis=1)
        high, low = split(y)
        u = dot(high, inner_ref[2]) + (dot(low, inner_ref[2]) + dot(high, inner_ref[3]))
        for c in range(0, 8, 2):
            one, two = u[64 * c : 64 * c + 64], u[64 * c + 64 : 64 * c + 128]
            ur = jnp.concatenate([one[:, :128], two[:, :128]], axis=1)
            ui = jnp.concatenate([one[:, 128:], two[:, 128:]], axis=1)
            w = jnp.concatenate([ur * cos_t - ui * sin_t, ui * cos_t + ur * sin_t], axis=0)
            high, low = split(w)
            y = dot(last_ref[...], jnp.concatenate([high, high], axis=0)) + dot(last_ref[:, :128], low)
            mixed[pl.ds(c, LEN_A, stride=8), :] = y[:, :128]
            mixed[pl.ds(c + 1, LEN_A, stride=8), :] = y[:, 128:]

    def put_mixed(q):
        gain_col = my_taps[8 * q : 8 * q + 8, 9:10]
        gain_col = jnp.concatenate([gain_col] * 8, axis=0)

        def four_blocks(j, carry):
            ended, tiles = carry
            here = pl.ds(pl.multiple_of(j * 64, 64), 64)
            y = mixed[here, :]
            high, low = split(y + gain_col * sig_t[q, here, :])
            found = dot(jnp.concatenate([high, low], axis=1), spots)
            for u in range(8):
                ended = ended + jnp.where(end_half == 8 * j + u, found[8 * u : 8 * u + 8], 0.0)
            for u in range(4):
                block = y[16 * u : 16 * u + 16]
                step = row_scale(jnp.maximum(jnp.abs(block[:8]), jnp.abs(block[8:])), 1)
                both = jnp.concatenate([step, step], axis=0)
                m_send[4 * j + u, CH * q : CH * q + CH] = code(block * (1.0 / both))
                tiles = jnp.where(lane == 32 + 4 * j + u, step, tiles)
            return ended, tiles

        empty = jnp.zeros((8, 128), F32)
        return lax.fori_loop(0, N_CTX // 4, four_blocks, (empty, empty), unroll=2)

    def turn(received):
        tmp[...] = received[...].reshape(N_CTX * CH, 128).astype(F32).T

    await_bytes(s_recv.at[pl.ds(0, N_CTX - 1), half[0]], recv_sem.at[3])
    convolve(0)
    ended0, tiles0 = put_mixed(0)
    send_half(6, 0, m_send, m_recv)

    await_bytes(s_recv.at[pl.ds(0, N_CTX - 1), half[1]], recv_sem.at[10])
    convolve(1)
    ended1, tiles1 = put_mixed(1)
    ended = q_end * jnp.concatenate([ended0, ended1], axis=0)
    tiles = jnp.concatenate([tiles0, tiles1], axis=0)
    lane = iota((CH, 128), 1)
    for g in range(4):
        turned = pltpu.roll(ended, (128 - 32 * g) % 128, 1)
        moved = pltpu.roll(tiles, (128 - 8 * g) % 128, 1)
        l_send[g] = jnp.where(lane < 32, turned, moved).astype(BF16)
    send_ctx(5, lambda peer: l_send.at[peer // 8], l_recv)
    l_recv[me] = l_send[me // 8]

    await_bytes(others(e_recv), recv_sem.at[4])
    turn(e_recv)
    ge_recv[rep, ch] = tmp[pl.ds(pl.multiple_of(lax.rem(me, 4) * 32, 32), 32), :].astype(BF16)
    send_ch(7, ge_recv)

    send_half(11, 1, m_send, m_recv)
    m_recv[me] = m_send[me]

    await_bytes(seven(ge_recv), recv_sem.at[7])
    swap_e = remote(12, ge_recv.at[rep], ge_recv.at[rep], sibling)
    swap_e.start()

    await_bytes(others(l_recv), recv_sem.at[5])
    turn(l_recv)
    four = tmp[pl.ds(pl.multiple_of(my_z // 2 * 8, 8), 8), :]
    four = jnp.where(lax.rem(my_z, 2) == 0, four[:4], four[4:])
    gl_recv[mine_near] = jnp.concatenate(
        [four[:, 128 * g : 128 * g + 128] for g in range(4)], axis=0
    ).astype(BF16)
    send_near(8, gl_recv)
    scales = tmp[32:40, :]
    m_steps = jnp.sum(jnp.where(iota((8, 512), 0) == my_z, scales, 0.0), axis=0, keepdims=True)

    await_bytes(m_recv.at[pl.ds(0, N_CTX - 1), half[0]], recv_sem.at[6])
    await_bytes(m_recv.at[pl.ds(0, N_CTX - 1), half[1]], recv_sem.at[11])
    gain = gain_ref[...]

    for g in range(4):
        here = slice(128 * g, 128 * g + 128)
        codes = decode(m_recv[8 * g : 8 * g + 8])
        for h in range(2):
            rows = slice(128 * h, 128 * h + 128)
            parts = [codes[:, CH * q + 8 * h : CH * q + 8 * h + 8] for q in range(2)]
            value = jnp.concatenate(parts, axis=1).reshape(128, 128).T * m_steps[:, here]
            out_ref[rows, here] = (
                query[rows, here] * (value + gain[:, here] * signal[rows, here])
            ).astype(BF16)

    swap_e.wait_recv()
    for c in range(8):
        for r in range(2):
            lanes = slice(512 * (2 * c + r), 512 * (2 * c + r) + 512)
            rows = ge_recv[r, c].astype(F32)
            for k in range(6):
                states_ref[k, :, lanes] = rows[4 * k : 4 * k + 4].astype(BF16)
    await_bytes(gl_recv.at[pl.ds(0, 15)], recv_sem.at[8])
    for j in range(16):
        rows = gl_recv[j].astype(F32)
        for g in range(4):
            first_lane = 512 * j + 128 * g
            states_ref[6, :, first_lane : first_lane + 128] = rows[4 * g : 4 * g + 4].astype(BF16)

    halo_copy.wait_send()
    for n, buffer in ((1, f_recv), (2, r_recv), (4, e_recv), (5, l_recv), (9, step_recv)):
        await_bytes(others(buffer), send_sem.at[n])
    for n, buffer in ((3, s_recv), (6, m_recv), (10, s_recv), (11, m_recv)):
        await_bytes(buffer.at[pl.ds(0, N_CTX - 1), half[0]], send_sem.at[n])
    await_bytes(seven(ge_recv), send_sem.at[7])
    await_bytes(gl_recv.at[pl.ds(0, 15)], send_sem.at[8])
    swap_e.wait_send()


def body(projections, short_taps, skip_gain, long_filter, request_ends, replica_of, slot_index):
    first, last, inner, turns = tables()
    whole = pl.BlockSpec(memory_space=pltpu.VMEM)
    operands = (
        projections, long_filter, short_taps, skip_gain.reshape(1, 512),
        request_ends.reshape(1, 128), replica_of.reshape(1, 128), slot_index.reshape(1, 128),
        jnp.asarray(first), jnp.asarray(last), jnp.asarray(inner), jnp.asarray(turns),
    )
    codes = pltpu.VMEM((N_CTX, 2 * CH, 128), jnp.int16)
    tiles = pltpu.VMEM((N_CTX, CH, 128), BF16)
    values = pltpu.VMEM((2, 512, 128), F32)
    tokens = pltpu.VMEM((TOK, 512), F32)
    output, states = pl.pallas_call(
        kernel,
        out_shape=(
            pltpu.VMEM((TOK, 512), BF16),
            pltpu.VMEM((7, SLOTS, 8192), BF16),
        ),
        in_specs=[pl.BlockSpec(memory_space=pltpu.HBM)] * len(operands),
        out_specs=(whole, whole),
        scratch_shapes=[
            *[pltpu.VMEM(x.shape, x.dtype) for x in operands],
            pltpu.VMEM((8, 512), F32), pltpu.VMEM((8, 512), F32),
            pltpu.VMEM((4, 1, 128), F32), pltpu.VMEM((N_CTX, 1, 128), F32),
            codes, codes, codes, tiles,
            pltpu.VMEM((8, CH, 128), BF16), pltpu.VMEM((4, CH, 128), BF16),
            codes, codes, codes, tiles, tiles, tiles,
            pltpu.VMEM((2, 8, 32, 512), BF16), pltpu.VMEM((16, 16, 128), BF16),
            pltpu.VMEM((2, 512, 256), F32),
            values, values, pltpu.VMEM((512, 128), F32), tokens, tokens,
            pltpu.VMEM((8, 512), F32),
            pltpu.VMEM((128, 1408), BF16),
            pltpu.VMEM((512, 16), F32),
            pltpu.VMEM((128, 512), F32),
            pltpu.SemaphoreType.DMA((11,)),
            pltpu.SemaphoreType.DMA((13,)),
            pltpu.SemaphoreType.DMA((13,)),
        ],
        compiler_params=pltpu.CompilerParams(
            collective_id=0, has_side_effects=True, vmem_limit_bytes=63 * 2**20
        ),
        cost_estimate=pl.CostEstimate(flops=2 * 10**9, bytes_accessed=4 * 10**6, transcendentals=0),
    )(*operands)
    return output, states.transpose(1, 0, 2)


def solution(mesh):
    return jax.shard_map(
        body,
        mesh=mesh,
        in_specs=(
            P(None, "ctx", ("ch", "rep")),
            P(None, None, ("ch", "rep")),
            P(("ch", "rep")),
            P("ctx", ("ch", "rep")),
            P(),
            P(),
            P(),
        ),
        out_specs=(P("ctx", ("ch", "rep")), P("ctx", None, None)),
        check_vma=False,
    )
```

```python
import math

import jax
import jax.numpy as jnp
import ml_dtypes
import numpy as np
from jax import lax
from jax.experimental import pallas as pl
from jax.experimental.pallas import tpu as pltpu
from jax.sharding import PartitionSpec as P

MESH = pl.DeviceIdType.MESH
F32 = jnp.float32
BF16 = jnp.bfloat16

N_CTX = 32
CH = 16
TOK = 256
SEQ = 8192
LEN_A = 64
LEN_B = 128
SLOTS = 4
TOP = 32767.0


def split_np(table):
    high = table.astype(ml_dtypes.bfloat16)
    low = (table - high.astype(np.float64)).astype(ml_dtypes.bfloat16)
    return high, low


def tables():
    k = np.arange(LEN_A) + 0.25
    theta = 2.0 * np.pi * np.outer(k, np.arange(LEN_A)) / LEN_A
    outer = np.concatenate([np.cos(theta), -np.sin(theta)], axis=0)
    o_high, o_low = split_np(outer)
    first = np.concatenate([o_high, o_high, o_low], axis=1)
    e_high, e_low = split_np(outer.T / SEQ)
    last = np.concatenate([e_high, e_low], axis=1)
    phi = 2.0 * np.pi * np.outer(np.arange(LEN_B), np.arange(LEN_B)) / LEN_B
    c, s = np.cos(phi), np.sin(phi)
    inner = np.block([[c, -s], [s, c]])
    i_high, i_low = split_np(inner)
    v_high, v_low = split_np(inner.T)
    inner_all = np.stack([i_high, i_low, v_high, v_low])
    turn = 2.0 * np.pi * np.outer(k, np.arange(LEN_B)) / SEQ
    turns = np.stack([np.tile(np.cos(turn), (1, 2)), np.tile(np.sin(turn), (1, 2))]).astype(np.float32)
    return first, last, inner_all, turns


def row_scale(block, axis):
    largest = jnp.max(jnp.abs(block), axis=axis, keepdims=True)
    step = jnp.maximum(largest, 2.0**-100) * (1.0078125 / TOP)
    return step.astype(BF16).astype(F32)


def code(scaled):
    return jnp.floor(scaled + 0.5).astype(jnp.int32).astype(jnp.int16)


def decode(codes):
    return codes.astype(jnp.int32).astype(F32)


def iota(shape, axis):
    return lax.broadcasted_iota(jnp.int32, shape, axis)


def split(value):
    high = value.astype(BF16)
    return high, (value - high.astype(F32)).astype(BF16)


def dot(a, b):
    return jnp.dot(a, b, preferred_element_type=F32)


def kernel(*refs):
    hbm_refs, (out_ref, states_ref), vmem_refs = refs[:11], refs[11:13], refs[13:24]
    (
        proj, filt, taps_ref, gain_ref, ends_ref, repl_ref, slot_ref,
        first_ref, last_ref, inner_ref, turns_ref,
    ) = vmem_refs
    (
        halo_send, halo_recv, step_send, step_recv, f_send, s_send, m_send, r_send, e_send, l_send,
        f_recv, s_recv, m_recv, r_recv, e_recv, l_recv, ge_recv, gl_recv,
        spec, filter_t, sig_t, mixed, query, signal, steps, onehot, taps_t, tmp,
        local_sem, send_sem, recv_sem,
    ) = refs[24:]
    me = lax.axis_index("ctx")
    ch, rep = lax.axis_index("ch"), lax.axis_index("rep")
    my_x, my_z = me // 8, lax.rem(me, 8)
    after = {"ctx": lax.rem(me + 1, N_CTX)}
    sibling = {"rep": 1 - rep}

    loads = [
        pltpu.make_async_copy(source, target, local_sem.at[n])
        for n, (source, target) in enumerate(zip(hbm_refs, vmem_refs))
    ]
    for load in loads:
        load.start()

    barrier = pltpu.get_barrier_semaphore()

    def greet(device):
        pl.semaphore_signal(barrier, inc=1, device_id=device, device_id_type=MESH)

    def greet_ctx(t, carry):
        greet({"ctx": lax.rem(me + t, N_CTX)})
        return carry

    mine_near = ch * 2 + rep

    def near(t):
        other = lax.rem(mine_near + t, 16)
        return {"ch": other // 2, "rep": lax.rem(other, 2)}

    def greet_near(t, carry):
        greet(near(t))
        return carry

    lax.fori_loop(1, N_CTX, greet_ctx, 0)
    lax.fori_loop(1, 16, greet_near, 0)

    def remote(n, source, target, device):
        return pltpu.make_async_remote_copy(
            src_ref=source, dst_ref=target,
            send_sem=send_sem.at[n], recv_sem=recv_sem.at[n],
            device_id=device, device_id_type=MESH,
        )

    def send_line(n, source, target, dx):
        x = lax.rem(my_x + dx, 4)

        def one(t, carry):
            peer = 8 * x + lax.rem(my_z + t, 8)
            remote(n, source(peer), target.at[me], {"ctx": peer}).start()
            return carry

        lax.fori_loop(1 if dx == 0 else 0, 8, one, 0)

    def send_ctx(n, source, target):
        for dx in range(4):
            send_line(n, source, target, dx)

    def send_ch(n, buffer):
        def one(t, carry):
            remote(n, buffer.at[rep, ch], buffer.at[rep, ch], {"ch": lax.rem(ch + t, 8)}).start()
            return carry

        lax.fori_loop(1, 8, one, 0)

    def send_near(n, buffer):
        def one(t, carry):
            remote(n, buffer.at[mine_near], buffer.at[mine_near], near(t)).start()
            return carry

        lax.fori_loop(1, 16, one, 0)

    def await_bytes(part, sem):
        pltpu.make_async_copy(part, part, sem).wait()

    def others(buffer):
        return buffer.at[pl.ds(0, N_CTX - 1)]

    def seven(buffer):
        return buffer.at[0, pl.ds(0, 7)]

    def column_block(dx):
        g = lax.rem(my_x + dx, 4)
        return pl.ds(pl.multiple_of(8 * g, 8), 8), pl.ds(pl.multiple_of(128 * g, 128), 128)

    def put_codes(block, kind, dx, target):
        devices, lanes = column_block(dx)
        step = row_scale(block, 0)
        steps[kind : kind + 1, lanes] = step
        turned = (block * (1.0 / step)).T.reshape(8, CH, TOK)
        parts = [
            turned[:, 8 * q : 8 * q + 8, 128 * h : 128 * h + 128] for q in range(2) for h in range(2)
        ]
        target[devices] = code(jnp.concatenate(parts, axis=1))

    def put_filter(dx):
        lanes = column_block(dx)[1]
        put_codes(filt[:, lanes], 0, dx, f_send)
        step_send[lax.rem(my_x + dx, 4)] = steps[0:1, lanes]

    loads[0].wait()
    halo_send[...] = jnp.concatenate(
        [proj[p, TOK - 16 :, :].astype(F32)[14:] for p in range(3)] + [jnp.zeros((2, 512), F32)], axis=0
    )
    steps[...] = jnp.zeros((8, 512), F32)
    loads[1].wait()
    put_filter(0)
    pl.semaphore_wait(barrier, N_CTX - 1 + 15)
    halo_copy = remote(0, halo_send, halo_recv, after)
    halo_copy.start()
    for dx in range(4):
        if dx > 0:
            put_filter(dx)
        send_line(1, lambda peer: f_send.at[peer], f_recv, dx)
        send_line(9, lambda peer: step_send.at[peer // 8], step_recv, dx)
    f_recv[me] = f_send[me]
    step_recv[me] = step_send[me // 8]
    for load in loads[2:]:
        load.wait()

    ends = ends_ref[...]
    end_block = ends // TOK
    end_lane = ends - end_block * TOK

    def down(row):
        return jnp.broadcast_to(row, (128, 128)).T

    earlier = iota((128, 128), 0) < iota((128, 128), 1)
    same = down(end_block) == end_block
    rank = jnp.sum(jnp.where(earlier, jnp.where(same, 1, 0), 0), axis=0, keepdims=True)
    slot_of = down(repl_ref[...] * SLOTS + slot_ref[...])

    def at_slot(row, slots):
        values = down(row)[:, :1]
        hit = slot_of[:, :1] == slots
        return jnp.sum(jnp.where(hit, values, 0), axis=0, keepdims=True)

    where_code = end_block * 16 + rank
    column = iota((128, 1024), 1)
    e_code = at_slot(where_code, column // 32 * 4 + column % 4)
    slots_row = iota((128, 128), 1)
    t_code = at_slot(where_code, slots_row)
    t_end = at_slot(ends, slots_row)
    row_kind = iota((1, 1024), 1) % 32 // 4
    code_all = jnp.concatenate([e_code, t_code, t_code, t_code], axis=1)
    kind_all = jnp.concatenate(
        [jnp.where(row_kind < 6, row_kind + 1, -10)] + [jnp.full((1, 128), k, jnp.int32) for k in range(3)],
        axis=1,
    )
    block_all = code_all // 16
    lane_all = kind_all * 16 + (code_all - block_all * 16)
    onehot[...] = jnp.where(iota((128, 1408), 0) == lane_all, 1.0, 0.0).astype(BF16)

    mine = jnp.where(end_block == me, jnp.where(rank == iota((16, 128), 0), end_lane + 100, 0), 0)
    place = jnp.sum(mine, axis=1, keepdims=True) - 100
    token = iota((16, TOK), 1)

    def rows_at(back):
        return jnp.where(token == place - back, 1.0, 0.0).astype(BF16)

    two_rows = jnp.concatenate([rows_at(1), rows_at(0)], axis=0)
    three_rows = jnp.concatenate([rows_at(2), two_rows], axis=0)

    halo_copy.wait_recv()
    token_row = iota((TOK, 128), 0)
    for dx in range(4):
        devices, lanes = column_block(dx)
        conv = []
        halo_here = jnp.where(me > 0, halo_recv[:, lanes], 0.0)
        for p in range(3):
            x = proj[p, :, lanes].astype(F32)
            tail2, tail1 = halo_here[2 * p : 2 * p + 1], halo_here[2 * p + 1 : 2 * p + 2]
            back1 = jnp.where(token_row < 1, tail1, pltpu.roll(x, 1, 0))
            back2 = jnp.where(
                token_row < 1, tail2, jnp.where(token_row < 2, tail1, pltpu.roll(x, 2, 0))
            )
            taps = taps_ref[p, :, lanes]
            conv.append(taps[0:1] * x + taps[1:2] * back1 + taps[2:3] * back2)
        query[:, lanes] = conv[0]
        product = conv[1] * conv[2]
        signal[:, lanes] = product
        put_codes(product, 1, dx, s_send)
        q_rows = dot(three_rows, proj[0, :, lanes])
        first_rows = q_rows[:16] + jnp.where(place == 1, halo_here[1:2], 0.0)
        rows = jnp.concatenate(
            [
                first_rows, q_rows[16:], dot(two_rows, proj[1, :, lanes]), dot(two_rows, proj[2, :, lanes]),
                steps[:, lanes], jnp.zeros((8, 128), F32),
            ],
            axis=0,
        )
        r_send[devices] = rows.T.astype(BF16).reshape(8, CH, 128)
        send_line(2, lambda peer: r_send.at[peer], r_recv, dx)
    r_recv[me] = r_send[me]
    half = [pl.ds(CH * q, CH) for q in range(2)]

    def send_half(n, q, source, target):
        for dx in range(4):
            x = lax.rem(my_x + dx, 4)

            def one(t, carry):
                peer = 8 * x + lax.rem(my_z + t, 8)
                remote(n, source.at[peer, half[q]], target.at[me, half[q]], {"ctx": peer}).start()
                return carry

            lax.fori_loop(1 if dx == 0 else 0, 8, one, 0)

    send_half(3, 0, s_send, s_recv)
    send_half(10, 1, s_send, s_recv)
    s_recv[me] = s_send[me]

    rows = [taps_ref[p] for p in range(3)] + [gain_ref[...], jnp.zeros((6, 512), F32)]
    taps_t[...] = jnp.concatenate(rows, axis=0).T
    my_taps = taps_t[pl.ds(pl.multiple_of(me * CH, CH), CH), :]

    cos_t, sin_t = turns_ref[0], turns_ref[1]

    def read_codes(received, q, step_of, target):
        for i in range(N_CTX):
            step = step_of(i)[8 * q : 8 * q + 8]
            step = jnp.concatenate([step, step], axis=0)
            target[q, 16 * i : 16 * i + 16, :] = decode(received[i, CH * q : CH * q + CH, :]) * step

    def forward(ref):
        turned = []
        for c in range(0, 8, 2):
            x = jnp.concatenate([ref[pl.ds(c + n, LEN_A, stride=8), :] for n in range(2)], axis=1)
            high, low = split(x)
            z = dot(first_ref[...], jnp.concatenate([high, low, high], axis=0))
            re, im = z[:64], z[64:]
            zr = re * cos_t + im * sin_t
            zi = im * cos_t - re * sin_t
            for n in (slice(0, 128), slice(128, 256)):
                turned.append(jnp.concatenate([zr[:, n], zi[:, n]], axis=1))
        high, low = split(jnp.concatenate(turned, axis=0))
        return dot(high, inner_ref[0]) + (dot(low, inner_ref[0]) + dot(high, inner_ref[1]))

    await_bytes(others(f_recv), recv_sem.at[1])
    await_bytes(others(step_recv), recv_sem.at[9])
    tmp[:, :32] = step_recv[...].reshape(N_CTX, 128).T
    f_steps = tmp[pl.ds(pl.multiple_of(my_z * CH, CH), CH), :32]
    for q in range(2):
        read_codes(f_recv, q, lambda i: f_steps[:, i : i + 1], filter_t)
        spec[q] = forward(filter_t.at[q])

    await_bytes(others(r_recv), recv_sem.at[2])
    def gather_four(i, total):
        blocks = r_recv[pl.ds(pl.multiple_of(4 * i, 4), 4)].reshape(4 * CH, 128)
        found = dot(blocks, onehot[...])
        for u in range(4):
            total = total + jnp.where(block_all == 4 * i + u, found[CH * u : CH * u + CH], 0.0)
        return total

    wanted = lax.fori_loop(0, N_CTX // 4, gather_four, jnp.zeros((CH, 1408), F32))
    for g in range(8):
        e_send[g] = wanted[:, 128 * g : 128 * g + 128].astype(BF16)
    send_ctx(4, lambda peer: e_send.at[peer // 4], e_recv)
    e_recv[me] = e_send[me // 4]
    q_end = (
        my_taps[:, 2:3] * wanted[:, 1024:1152]
        + my_taps[:, 1:2] * wanted[:, 1152:1280]
        + my_taps[:, 0:1] * wanted[:, 1280:1408]
    )

    lane = iota((8, 128), 1)
    end_half = t_end // 128
    end_spot = t_end - end_half * 128
    spot = jnp.where(iota((128, 128), 0) == end_spot, 1.0, 0.0).astype(BF16)
    spots = jnp.concatenate([spot, spot], axis=0)

    def convolve(q):
        read_codes(s_recv, q, lambda i: r_recv[i].astype(F32)[:, 113:114], sig_t)
        x, f = forward(sig_t.at[q]), spec[q]
        xr, xi, fr, fi = x[:, :128], x[:, 128:], f[:, :128], f[:, 128:]
        y = jnp.concatenate([xr * fr - xi * fi, xr * fi + xi * fr], axis=1)
        high, low = split(y)
        u = dot(high, inner_ref[2]) + (dot(low, inner_ref[2]) + dot(high, inner_ref[3]))
        for c in range(0, 8, 2):
            one, two = u[64 * c : 64 * c + 64], u[64 * c + 64 : 64 * c + 128]
            ur = jnp.concatenate([one[:, :128], two[:, :128]], axis=1)
            ui = jnp.concatenate([one[:, 128:], two[:, 128:]], axis=1)
            w = jnp.concatenate([ur * cos_t - ui * sin_t, ui * cos_t + ur * sin_t], axis=0)
            high, low = split(w)
            y = dot(last_ref[...], jnp.concatenate([high, high], axis=0)) + dot(last_ref[:, :128], low)
            mixed[pl.ds(c, LEN_A, stride=8), :] = y[:, :128]
            mixed[pl.ds(c + 1, LEN_A, stride=8), :] = y[:, 128:]

    def put_mixed(q):
        gain_col = my_taps[8 * q : 8 * q + 8, 9:10]
        gain_col = jnp.concatenate([gain_col] * 8, axis=0)

        def four_blocks(j, carry):
            ended, tiles = carry
            here = pl.ds(pl.multiple_of(j * 64, 64), 64)
            y = mixed[here, :]
            high, low = split(y + gain_col * sig_t[q, here, :])
            found = dot(jnp.concatenate([high, low], axis=1), spots)
            for u in range(8):
                ended = ended + jnp.where(end_half == 8 * j + u, found[8 * u : 8 * u + 8], 0.0)
            for u in range(4):
                block = y[16 * u : 16 * u + 16]
                step = row_scale(jnp.maximum(jnp.abs(block[:8]), jnp.abs(block[8:])), 1)
                both = jnp.concatenate([step, step], axis=0)
                m_send[4 * j + u, CH * q : CH * q + CH] = code(block * (1.0 / both))
                tiles = jnp.where(lane == 32 + 4 * j + u, step, tiles)
            return ended, tiles

        empty = jnp.zeros((8, 128), F32)
        return lax.fori_loop(0, N_CTX // 4, four_blocks, (empty, empty), unroll=2)

    def turn(received):
        tmp[...] = received[...].reshape(N_CTX * CH, 128).astype(F32).T

    await_bytes(s_recv.at[pl.ds(0, N_CTX - 1), half[0]], recv_sem.at[3])
    convolve(0)
    ended0, tiles0 = put_mixed(0)
    send_half(6, 0, m_send, m_recv)

    await_bytes(s_recv.at[pl.ds(0, N_CTX - 1), half[1]], recv_sem.at[10])
    convolve(1)
    ended1, tiles1 = put_mixed(1)
    ended = q_end * jnp.concatenate([ended0, ended1], axis=0)
    tiles = jnp.concatenate([tiles0, tiles1], axis=0)
    lane = iota((CH, 128), 1)
    for g in range(4):
        turned = pltpu.roll(ended, (128 - 32 * g) % 128, 1)
        moved = pltpu.roll(tiles, (128 - 8 * g) % 128, 1)
        l_send[g] = jnp.where(lane < 32, turned, moved).astype(BF16)
    send_ctx(5, lambda peer: l_send.at[peer // 8], l_recv)
    l_recv[me] = l_send[me // 8]

    await_bytes(others(e_recv), recv_sem.at[4])
    turn(e_recv)
    ge_recv[rep, ch] = tmp[pl.ds(pl.multiple_of(lax.rem(me, 4) * 32, 32), 32), :].astype(BF16)
    send_ch(7, ge_recv)

    send_half(11, 1, m_send, m_recv)
    m_recv[me] = m_send[me]

    await_bytes(others(l_recv), recv_sem.at[5])
    turn(l_recv)
    four = tmp[pl.ds(pl.multiple_of(my_z // 2 * 8, 8), 8), :]
    four = jnp.where(lax.rem(my_z, 2) == 0, four[:4], four[4:])
    gl_recv[mine_near] = jnp.concatenate(
        [four[:, 128 * g : 128 * g + 128] for g in range(4)], axis=0
    ).astype(BF16)
    send_near(8, gl_recv)

    await_bytes(seven(ge_recv), recv_sem.at[7])
    swap_e = remote(12, ge_recv.at[rep], ge_recv.at[rep], sibling)
    swap_e.start()

    scales = tmp[32:40, :]
    m_steps = jnp.sum(jnp.where(iota((8, 512), 0) == my_z, scales, 0.0), axis=0, keepdims=True)

    await_bytes(m_recv.at[pl.ds(0, N_CTX - 1), half[0]], recv_sem.at[6])
    await_bytes(m_recv.at[pl.ds(0, N_CTX - 1), half[1]], recv_sem.at[11])
    gain = gain_ref[...]

    for g in range(4):
        here = slice(128 * g, 128 * g + 128)
        codes = decode(m_recv[8 * g : 8 * g + 8])
        for h in range(2):
            rows = slice(128 * h, 128 * h + 128)
            parts = [codes[:, CH * q + 8 * h : CH * q + 8 * h + 8] for q in range(2)]
            value = jnp.concatenate(parts, axis=1).reshape(128, 128).T * m_steps[:, here]
            out_ref[rows, here] = (
                query[rows, here] * (value + gain[:, here] * signal[rows, here])
            ).astype(BF16)

    swap_e.wait_recv()
    for c in range(8):
        for r in range(2):
            lanes = slice(512 * (2 * c + r), 512 * (2 * c + r) + 512)
            rows = ge_recv[r, c].astype(F32)
            for k in range(6):
                states_ref[k, :, lanes] = rows[4 * k : 4 * k + 4].astype(BF16)
    await_bytes(gl_recv.at[pl.ds(0, 15)], recv_sem.at[8])
    for j in range(16):
        rows = gl_recv[j].astype(F32)
        for g in range(4):
            first_lane = 512 * j + 128 * g
            states_ref[6, :, first_lane : first_lane + 128] = rows[4 * g : 4 * g + 4].astype(BF16)

    halo_copy.wait_send()
    for n, buffer in ((1, f_recv), (2, r_recv), (4, e_recv), (5, l_recv), (9, step_recv)):
        await_bytes(others(buffer), send_sem.at[n])
    for n, buffer in ((3, s_recv), (6, m_recv), (10, s_recv), (11, m_recv)):
        await_bytes(buffer.at[pl.ds(0, N_CTX - 1), half[0]], send_sem.at[n])
    await_bytes(seven(ge_recv), send_sem.at[7])
    await_bytes(gl_recv.at[pl.ds(0, 15)], send_sem.at[8])
    swap_e.wait_send()


def body(projections, short_taps, skip_gain, long_filter, request_ends, replica_of, slot_index):
    first, last, inner, turns = tables()
    whole = pl.BlockSpec(memory_space=pltpu.VMEM)
    operands = (
        projections, long_filter, short_taps, skip_gain.reshape(1, 512),
        request_ends.reshape(1, 128), replica_of.reshape(1, 128), slot_index.reshape(1, 128),
        jnp.asarray(first), jnp.asarray(last), jnp.asarray(inner), jnp.asarray(turns),
    )
    codes = pltpu.VMEM((N_CTX, 2 * CH, 128), jnp.int16)
    tiles = pltpu.VMEM((N_CTX, CH, 128), BF16)
    values = pltpu.VMEM((2, 512, 128), F32)
    tokens = pltpu.VMEM((TOK, 512), F32)
    output, states = pl.pallas_call(
        kernel,
        out_shape=(
            pltpu.VMEM((TOK, 512), BF16),
            pltpu.VMEM((7, SLOTS, 8192), BF16),
        ),
        in_specs=[pl.BlockSpec(memory_space=pltpu.HBM)] * len(operands),
        out_specs=(whole, whole),
        scratch_shapes=[
            *[pltpu.VMEM(x.shape, x.dtype) for x in operands],
            pltpu.VMEM((8, 512), F32), pltpu.VMEM((8, 512), F32),
            pltpu.VMEM((4, 1, 128), F32), pltpu.VMEM((N_CTX, 1, 128), F32),
            codes, codes, codes, tiles,
            pltpu.VMEM((8, CH, 128), BF16), pltpu.VMEM((4, CH, 128), BF16),
            codes, codes, codes, tiles, tiles, tiles,
            pltpu.VMEM((2, 8, 32, 512), BF16), pltpu.VMEM((16, 16, 128), BF16),
            pltpu.VMEM((2, 512, 256), F32),
            values, values, pltpu.VMEM((512, 128), F32), tokens, tokens,
            pltpu.VMEM((8, 512), F32),
            pltpu.VMEM((128, 1408), BF16),
            pltpu.VMEM((512, 16), F32),
            pltpu.VMEM((128, 512), F32),
            pltpu.SemaphoreType.DMA((11,)),
            pltpu.SemaphoreType.DMA((13,)),
            pltpu.SemaphoreType.DMA((13,)),
        ],
        compiler_params=pltpu.CompilerParams(
            collective_id=0, has_side_effects=True, vmem_limit_bytes=63 * 2**20
        ),
        cost_estimate=pl.CostEstimate(flops=2 * 10**9, bytes_accessed=4 * 10**6, transcendentals=0),
    )(*operands)
    return output, states.transpose(1, 0, 2)


def solution(mesh):
    return jax.shard_map(
        body,
        mesh=mesh,
        in_specs=(
            P(None, "ctx", ("ch", "rep")),
            P(None, None, ("ch", "rep")),
            P(("ch", "rep")),
            P("ctx", ("ch", "rep")),
            P(),
            P(),
            P(),
        ),
        out_specs=(P("ctx", ("ch", "rep")), P("ctx", None, None)),
        check_vma=False,
    )
```
